32 devices in a mesh: dp: 2 (over x), ctx: 4 (over z), tp: 4 (over y, core).
Axes of the slice: x: 2, y: 2, z: 4, core: 2. Of those that a mesh axis runs over, the one named last changes fastest.
Arguments:
- query_proj: bfloat16 [2, 1024, 2048], P('dp', 'ctx', 'tp'), may hold values from -6 to 6
- key_proj: bfloat16 [2, 1024, 2048], P('dp', 'ctx', 'tp'), may hold values from -6 to 6
- value_proj: bfloat16 [2, 1024, 2048], P('dp', 'ctx', 'tp'), may hold values from -6 to 6
- filters: float32 [2048, 1024], P('tp', 'ctx'), may hold values from -2 to 2
- w_out: bfloat16 [2048, 2048], P('tp'), may hold values from -0.125 to 0.125
- cotangent: bfloat16 [2, 1024, 2048], P('dp', 'ctx', 'tp'), may hold values from -6 to 6
Outputs:
- output: bfloat16 [2, 1024, 2048], P('dp', 'ctx', 'tp')
- grad_query: bfloat16 [2, 1024, 2048], P('dp', 'ctx', 'tp')
- grad_key: bfloat16 [2, 1024, 2048], P('dp', 'ctx', 'tp')
- grad_value: bfloat16 [2, 1024, 2048], P('dp', 'ctx', 'tp')
- grad_filter: float32 [2048, 1024], P('tp', 'ctx')
- grad_wout: float32 [2048, 2048], P('tp', 'ctx')
The draws below stay inside these ranges and needn't reach their ends.
All inputs are finite; a program needn't handle non-finite values.
Results may differ from the reference program's by a relative error of at most 0.0049.
Values may be sent and summed in bfloat16 or wider, within the bound.
No kernel may reach another device: no remote copies, remote signals or barrier semaphores. Data moves between devices by JAX's collectives and lax.ppermute only.
A program may use at most 64 MiB of HBM per device.

```python
import math
import jax
import jax.numpy as jnp
from jax import lax

C = 2048
DOUT = 2048
BATCH = 2
L = 1024


def envelope_norm(rates, length):
    return jnp.sqrt(2.0 * rates / (1.0 - jnp.exp(-2.0 * rates * length)))


def draw_filters(key, part):
    key = jax.random.fold_in(key, 11)
    key_fast, key_slow, key_share, key_taps = jax.random.split(key, 4)
    fast_rates = jnp.exp(jax.random.uniform(key_fast, (C, 1), jnp.float32, math.log(1.0 / 400.0), math.log(1.0 / 40.0)))
    slow_rates = jnp.exp(jax.random.uniform(key_slow, (C, 1), jnp.float32, math.log(0.1 / L), math.log(1.5 / L)))
    slow_share = jax.random.uniform(key_share, (C, 1), jnp.float32, 0.3, 0.7)
    tap_index = jnp.arange(L, dtype=jnp.float32)[None, :]
    fast_part = jnp.exp(-fast_rates * tap_index) * envelope_norm(fast_rates, L) * jnp.sqrt(1.0 - slow_share)
    slow_part = jnp.exp(-slow_rates * tap_index) * envelope_norm(slow_rates, L) * jnp.sqrt(slow_share)
    envelope = fast_part + slow_part
    pattern = jnp.clip(jax.random.normal(key_taps, (C, L), jnp.float32), -5.0, 5.0)
    return jnp.clip(pattern * envelope, -2.0, 2.0).astype(jnp.float32)


def strengthened(drawn, rng, source, target, shards_of, factor):
    def block_of(dim):
        return (jnp.arange(drawn.shape[dim]) // (drawn.shape[dim] // shards_of)).reshape((-1,) + (1,) * (drawn.ndim - 1 - dim))

    one_side = jax.random.permutation(rng, shards_of)[block_of(target)]
    other_side = (block_of(target) + shards_of // 2) % shards_of
    return jnp.where((block_of(source) == one_side) | (block_of(source) == other_side), factor * drawn, drawn)


def block_scale(key, extent, cuts, least, top_value):
    loudness = 1.0
    for dim, parts in cuts:
        heights = jax.random.uniform(jax.random.fold_in(jax.random.fold_in(key, 6), dim), (parts,), jnp.float32, least / len(cuts), top_value / len(cuts))
        loudness = loudness * jnp.repeat(jnp.exp(heights), extent[dim] // parts).reshape((-1,) + (1,) * (len(extent) - 1 - dim))
    return loudness


def centred(stream_key, extent, deviation, most, pieces=(), held_as=jnp.bfloat16):
    drawn = jax.random.normal(stream_key, extent, jnp.float32) * deviation
    if len(pieces) > 0:
        drawn = block_scale(stream_key, extent, pieces, -0.22, 0.18) * drawn
    return jnp.clip(drawn, min=-most, max=most).astype(held_as)


def noise_with(key, shape, deviation, reach, cuts, heavy, held_as=jnp.bfloat16):
    array = deviation * jax.random.normal(key, shape, jnp.float32)
    if cuts:
        array = array * block_scale(key, shape, cuts, -0.22, 0.18)
    return jnp.clip(strengthened(array, jax.random.fold_in(key, 3), *heavy), -reach, reach).astype(held_as)


def setup_inputs(seed: int = 0) -> dict:
    key_list = jax.random.split(jax.random.key(seed), 7)
    return {
        "query_proj": centred(key_list[0], (BATCH, L, C), 1.0, 6.0, ((0, 2), (1, 4), (2, 4))),
        "key_proj": centred(key_list[1], (BATCH, L, C), 1.0, 6.0, ((0, 2), (1, 4), (2, 4))),
        "value_proj": centred(key_list[2], (BATCH, L, C), 1.0, 6.0, ((0, 2), (1, 4), (2, 4))),
        "filters": draw_filters(jax.random.fold_in(key_list[6], 71), 0),
        "w_out": centred(key_list[4], (C, DOUT), C ** -0.5, 0.125, ((0, 4),)),
        "cotangent": noise_with(key_list[5], (BATCH, L, DOUT), 1.0, 6.0, ((0, 2), (1, 4), (2, 4)), (1, 2, 4, 2.0)),
    }


def reference(query_proj, key_proj, value_proj, filters, w_out, cotangent):
    length = query_proj.shape[1]
    length_fft = 2 * length
    filter_spec = jnp.fft.rfft(filters, n=length_fft, axis=1)

    def one_sequence(inputs):
        query_rows, key_rows, value_rows, grad_rows = inputs
        mixed = (key_rows.astype(jnp.float32) * value_rows.astype(jnp.float32)).T
        mixed_spec = jnp.fft.rfft(mixed, n=length_fft, axis=1)
        conv = jnp.fft.irfft(filter_spec * mixed_spec, n=length_fft, axis=1)[:, :length].T.astype(jnp.float32)
        gated = (query_rows.astype(jnp.float32) * conv).astype(jnp.bfloat16)
        output = jnp.dot(gated, w_out, preferred_element_type=jnp.float32).astype(jnp.bfloat16)
        grad_gated = lax.dot_general(grad_rows, w_out, (((1,), (1,)), ((), ())), preferred_element_type=jnp.float32)
        grad_query = (grad_gated * conv).astype(jnp.bfloat16)
        grad_conv = (grad_gated * query_rows.astype(jnp.float32)).T
        grad_spec = jnp.fft.rfft(grad_conv, n=length_fft, axis=1)
        grad_mixed = jnp.fft.irfft(jnp.conj(filter_spec) * grad_spec, n=length_fft, axis=1)[:, :length].T.astype(jnp.float32)
        filter_term = jnp.fft.irfft(grad_spec * jnp.conj(mixed_spec), n=length_fft, axis=1)[:, :length].astype(jnp.float32)
        grad_key = (grad_mixed * value_rows.astype(jnp.float32)).astype(jnp.bfloat16)
        grad_value = (grad_mixed * key_rows.astype(jnp.float32)).astype(jnp.bfloat16)
        weight_term = lax.dot_general(gated, grad_rows, (((0,), (0,)), ((), ())), preferred_element_type=jnp.float32)
        return (output, grad_query, grad_key, grad_value, filter_term, weight_term)
    results = lax.map(one_sequence, (query_proj, key_proj, value_proj, cotangent))
    output, grad_query, grad_key, grad_value, filter_terms, weight_terms = results
    factor = 1.0 / math.sqrt(BATCH * L)
    grad_filter = lax.optimization_barrier(jnp.sum(filter_terms, axis=0)) * factor
    grad_wout = lax.optimization_barrier(jnp.sum(weight_terms, axis=0)) * factor
    return (output, grad_query, grad_key, grad_value, grad_filter, grad_wout)
```

```python
import functools
import math

import jax
import jax.numpy as jnp
import ml_dtypes
import numpy as np
from jax import lax
from jax.experimental import pallas as pl
from jax.experimental.pallas import tpu as pltpu
from jax.sharding import PartitionSpec as P

F32 = jnp.float32
BF16 = jnp.bfloat16
LANES = 128
ROWS = 16


def build_tables(length_fft):
    blocks = length_fft // 128
    outer = jnp.arange(blocks, dtype=jnp.int32)
    inner = jnp.arange(blocks // 2, dtype=jnp.int32)
    column = jnp.arange(128, dtype=jnp.int32)
    first = (outer[:, None] * inner[None, :] % blocks).astype(jnp.float32) * (
        -2.0 * math.pi / blocks
    )
    turned = (outer[:, None] * column[None, :] % length_fft).astype(jnp.float32) * (
        -2.0 * math.pi / length_fft
    )
    second = (column[:, None] * column[None, :] % 128).astype(jnp.float32) * (-2.0 * math.pi / 128)
    return (
        jnp.cos(first),
        jnp.sin(first),
        jnp.cos(turned),
        jnp.sin(turned),
        jnp.cos(second),
        jnp.sin(second),
    )


def product(form, left, right):
    return jnp.einsum(form, left, right, precision=lax.Precision.HIGHEST)


def forward_transform(signal, tables):
    cos_first, sin_first, cos_turn, sin_turn, cos_second, sin_second = tables
    real_one = product("ia,cab->cib", cos_first, signal)
    imag_one = product("ia,cab->cib", sin_first, signal)
    real_two = real_one * cos_turn - imag_one * sin_turn
    imag_two = real_one * sin_turn + imag_one * cos_turn
    real_out = product("cib,bj->cij", real_two, cos_second) - product(
        "cib,bj->cij", imag_two, sin_second
    )
    imag_out = product("cib,bj->cij", real_two, sin_second) + product(
        "cib,bj->cij", imag_two, cos_second
    )
    return (real_out, imag_out)


def inverse_transform(real_in, imag_in, tables, length_fft):
    cos_first, sin_first, cos_turn, sin_turn, cos_second, sin_second = tables
    real_one = product("cij,jb->cib", real_in, cos_second) + product(
        "cij,jb->cib", imag_in, sin_second
    )
    imag_one = product("cij,jb->cib", imag_in, cos_second) - product(
        "cij,jb->cib", real_in, sin_second
    )
    real_two = real_one * cos_turn + imag_one * sin_turn
    imag_two = imag_one * cos_turn - real_one * sin_turn
    result = product("ia,cib->cab", cos_first, real_two) + product(
        "ia,cib->cab", sin_first, imag_two
    )
    return result / length_fft


def local_any_length(query_proj, key_proj, value_proj, filters, w_out, cotangent):
    query_rows = query_proj[0].astype(jnp.float32)
    key_rows = key_proj[0].astype(jnp.float32)
    value_rows = value_proj[0].astype(jnp.float32)
    positions, channels = query_rows.shape
    seq_devices = lax.axis_size("ctx")
    length_fft = 2 * positions * seq_devices
    tables = build_tables(length_fft)
    mixed = (key_rows * value_rows).T
    mixed_chan, filter_chan = (
        lax.all_to_all(mixed, "ctx", split_axis=0, concat_axis=1, tiled=True),
        lax.all_to_all(filters, "ctx", split_axis=0, concat_axis=1, tiled=True),
    )
    local_channels = mixed_chan.shape[0]
    block_shape = (local_channels, length_fft // 256, 128)
    mixed_real, mixed_imag = forward_transform(mixed_chan.reshape(block_shape), tables)
    filter_real, filter_imag = forward_transform(filter_chan.reshape(block_shape), tables)
    conv_real = filter_real * mixed_real - filter_imag * mixed_imag
    conv_imag = filter_real * mixed_imag + filter_imag * mixed_real
    conv_chan = inverse_transform(conv_real, conv_imag, tables, length_fft).reshape(
        local_channels, -1
    )
    conv_back = lax.all_to_all(conv_chan, "ctx", split_axis=1, concat_axis=0, tiled=True)
    conv = conv_back.T
    gated = (query_rows * conv).astype(jnp.bfloat16)
    partial_terms = jnp.dot(gated, w_out, preferred_element_type=jnp.float32)
    output = lax.psum_scatter(partial_terms, "tp", scatter_dimension=1, tiled=True).astype(
        jnp.bfloat16
    )
    piece = lax.all_gather(cotangent[0], "tp", axis=1, tiled=True)
    grad_gated = lax.dot_general(
        piece, w_out, (((1,), (1,)), ((), ())), preferred_element_type=jnp.float32
    )
    weight_piece = lax.dot_general(
        gated, piece, (((0,), (0,)), ((), ())), preferred_element_type=jnp.float32
    )
    weight_grad = weight_piece
    grad_gated, weight_grad = (grad_gated, weight_grad)
    grad_query = (grad_gated * conv).astype(jnp.bfloat16)
    grad_conv = (grad_gated * query_rows).T
    grad_chan = lax.all_to_all(grad_conv, "ctx", split_axis=0, concat_axis=1, tiled=True)
    grad_real, grad_imag = forward_transform(grad_chan.reshape(block_shape), tables)
    back_real = filter_real * grad_real + filter_imag * grad_imag
    back_imag = filter_real * grad_imag - filter_imag * grad_real
    taps_real = grad_real * mixed_real + grad_imag * mixed_imag
    taps_imag = grad_imag * mixed_real - grad_real * mixed_imag
    mixed_grad_chan = inverse_transform(back_real, back_imag, tables, length_fft).reshape(
        local_channels, -1
    )
    filter_grad_chan = inverse_transform(taps_real, taps_imag, tables, length_fft).reshape(
        local_channels, -1
    )
    mixed_grad_back, filter_grad_back = (
        lax.all_to_all(mixed_grad_chan, "ctx", split_axis=1, concat_axis=0, tiled=True),
        lax.all_to_all(filter_grad_chan, "ctx", split_axis=1, concat_axis=0, tiled=True),
    )
    grad_mixed = mixed_grad_back.T
    grad_key = (grad_mixed * value_rows).astype(jnp.bfloat16)
    grad_value = (grad_mixed * key_rows).astype(jnp.bfloat16)
    factor = 1.0 / math.sqrt(lax.axis_size("dp") * positions * seq_devices)
    grad_filter = lax.psum(filter_grad_back, "dp") * factor
    summed_seq = lax.psum_scatter(weight_grad, "ctx", scatter_dimension=1, tiled=True)
    summed_weight = lax.psum(summed_seq, "dp")
    grad_wout = summed_weight * factor
    return (
        output[None],
        grad_query[None],
        grad_key[None],
        grad_value[None],
        grad_filter,
        grad_wout,
    )


@functools.lru_cache
def transform_tables(blocks):
    length_fft = 2 * blocks * LANES
    b = np.arange(LANES, dtype=np.int64)
    angle = (2.0 * math.pi / LANES) * (b[:, None] * b[None, :] % LANES)
    cos, sin = np.cos(angle), np.sin(angle)
    whole = np.block([[cos, sin], [-sin, cos]])
    high = whole.astype(ml_dtypes.bfloat16)
    low = (whole - high.astype(np.float64)).astype(ml_dtypes.bfloat16)
    turn = np.zeros((LANES, LANES))
    i = np.arange(blocks + 1)
    angle = (2.0 * math.pi / length_fft) * (b[:, None] * i[None, :] % length_fft)
    turn[:, : blocks + 1] = np.cos(angle)
    turn[:, LANES // 2 : LANES // 2 + blocks + 1] = np.sin(angle)
    return np.stack([high, low]), turn.astype(np.float32)


def scaled_sum(terms):
    total = None
    for factor, term in terms:
        if abs(factor) < 1e-9:
            continue
        if abs(factor - 1.0) < 1e-9:
            total = term if total is None else total + term
        elif abs(factor + 1.0) < 1e-9:
            total = -term if total is None else total - term
        else:
            total = factor * term if total is None else total + factor * term
    return total


def split_bf16(value):
    high = value.astype(BF16)
    return high, (value - high.astype(F32)).astype(BF16)


def product3(matrix_ref, high, low):
    dot = functools.partial(jnp.dot, preferred_element_type=F32)
    return dot(matrix_ref[0], high) + (dot(matrix_ref[0], low) + dot(matrix_ref[1], high))


def turn_of(turn_ref, i, row):
    rows = pl.ds(row, ROWS)
    cos = turn_ref[rows, i : i + 1]
    sin = turn_ref[rows, LANES // 2 + i : LANES // 2 + i + 1]
    return jnp.broadcast_to(cos, (ROWS, LANES)), jnp.broadcast_to(sin, (ROWS, LANES))


def each_chunk(lanes, body):
    @pl.loop(0, LANES // ROWS)
    def _(step):
        for lane in range(0, lanes, LANES):
            body(pl.multiple_of(step * ROWS, ROWS), lane)


def over_blocks(read, blocks, lanes, turn_ref, high, low):
    def chunk(row, lane):
        def put(i, real, imag):
            if i > 0:
                cos, sin = turn_of(turn_ref, i, row)
                if imag is None:
                    real, imag = real * cos, -(real * sin)
                else:
                    real, imag = real * cos + imag * sin, imag * cos - real * sin
            for part, value in ((0, real), (1, jnp.zeros_like(real) if imag is None else imag)):
                top, rest = split_bf16(value)
                rows = pl.ds(pl.multiple_of(part * LANES + row, ROWS), ROWS)
                high[i, rows, pl.ds(lane, LANES)] = top
                low[i, rows, pl.ds(lane, LANES)] = rest

        slabs = [read(a, row, lane) for a in range(blocks)]
        for i in range(blocks // 2 + 1):
            sums = []
            for first in (0, 1):
                picked = range(first, blocks, 2)
                angle = [math.pi * ((i * a) % (2 * blocks)) / blocks for a in picked]
                sums.append(scaled_sum([(math.cos(g), slabs[a]) for g, a in zip(angle, picked)]))
                sums.append(scaled_sum([(-math.sin(g), slabs[a]) for g, a in zip(angle, picked)]))
            even_real, even_imag, odd_real, odd_imag = sums

            def joined(one, other, sign):
                if one is None or other is None:
                    return one if other is None else (other if sign > 0 else -other)
                return one + other if sign > 0 else one - other

            put(i, joined(even_real, odd_real, 1), joined(even_imag, odd_imag, 1))
            if blocks - i != i:
                put(blocks - i, joined(even_real, odd_real, -1), joined(odd_imag, even_imag, -1))

    each_chunk(lanes, chunk)


def back_to_blocks(turned, blocks, lanes, turn_ref, write):
    scale = 1.0 / (blocks * LANES)

    def chunk(row, lane):
        def get(i):
            real = turned[i, pl.ds(row, ROWS), pl.ds(lane, LANES)]
            imag = -turned[i, pl.ds(pl.multiple_of(LANES + row, ROWS), ROWS), pl.ds(lane, LANES)]
            if i > 0:
                cos, sin = turn_of(turn_ref, i, row)
                real, imag = real * cos - imag * sin, imag * cos + real * sin
            return real, imag

        terms = [[] for _ in range(blocks)]
        for i in range(blocks // 2 + 1):
            real, imag = get(i)
            if blocks - i != i:
                other_real, other_imag = get(blocks - i)
                pairs = ((real + other_real, imag - other_imag), (real - other_real, imag + other_imag))
            else:
                pairs = ((real, imag), (real, imag))
            if i == 0:
                pairs = tuple((0.5 * one, 0.5 * two) for one, two in pairs)
            for a in range(blocks):
                angle = math.pi * ((i * a) % (2 * blocks)) / blocks
                terms[a].append((math.cos(angle), pairs[a % 2][0]))
                terms[a].append((-math.sin(angle), pairs[a % 2][1]))
        for a in range(blocks):
            write(a, row, lane, scaled_sum(terms[a]) * scale)

    each_chunk(lanes, chunk)


def at_block(index, size=LANES):
    return pl.ds(pl.multiple_of(index * size, size), size)


def reader(ref):
    def read(a, row, lane):
        rows = pl.ds(pl.multiple_of(a * LANES + row, ROWS), ROWS)
        return ref[rows, pl.ds(lane, LANES)].astype(F32)

    return read


def writer(ref):
    def write(a, row, lane, value):
        rows = pl.ds(pl.multiple_of(a * LANES + row, ROWS), ROWS)
        ref[rows, pl.ds(lane, LANES)] = value.astype(ref.dtype)

    return write


def place_pieces(pieces, whole):
    me = lax.axis_index("ctx")
    for r, ref in enumerate(pieces):
        whole[at_block(me ^ r, ref.shape[0]), :] = ref[...]


def take_pieces(whole, pieces):
    me = lax.axis_index("ctx")
    for r, ref in enumerate(pieces):
        ref[...] = whole[at_block(me ^ r, ref.shape[0]), :]


def fetch(pairs, sems):
    copies = [pltpu.make_async_copy(source, target, sems.at[n]) for n, (source, target) in enumerate(pairs)]
    for copy in copies:
        copy.start()
    return copies


def prepare_kernel(*refs):
    *pieces, key_ref, value_ref, filter_ref, sems = refs[3:]
    for copy in fetch(list(zip(refs[:3], (key_ref, value_ref, filter_ref))), sems):
        copy.wait()
    me = lax.axis_index("ctx")
    for r, out_ref in enumerate(pieces):
        cols = at_block(me ^ r)
        mixed = key_ref[:, cols].astype(F32) * value_ref[:, cols].astype(F32)
        out_ref[:, pl.ds(0, LANES)] = mixed.astype(BF16)
        out_ref[:, pl.ds(LANES, LANES)] = filter_ref[cols, :].T.astype(BF16)


def forward_kernel(seqs, *refs):
    held, (matrix, turn, moved_ref), refs = refs[:seqs], refs[seqs : seqs + 3], refs[seqs + 4 :]
    sent, (spec_ref, passed_ref, whole, zh, zl, turned, conv) = refs[:seqs], refs[seqs:]
    blocks = spec_ref.shape[0] - 1
    passed_ref[...] = moved_ref[...]
    place_pieces(held, whole)
    over_blocks(reader(whole), blocks, 2 * LANES, turn, zh, zl)
    for i in range(blocks + 1):
        spec = product3(matrix, zh[i], zl[i])
        spec_ref[i] = spec
        mixed_real, mixed_imag = spec[:LANES, :LANES], spec[LANES:, :LANES]
        filter_real, filter_imag = spec[:LANES, LANES:], spec[LANES:, LANES:]
        real = filter_real * mixed_real - filter_imag * mixed_imag
        imag = filter_real * mixed_imag + filter_imag * mixed_real
        turned[i] = product3(matrix, *split_bf16(jnp.concatenate([real, -imag], axis=0)))
    back_to_blocks(turned, blocks, LANES, turn, writer(conv))
    take_pieces(conv, sent)


def backward_kernel(seqs, *refs):
    held, (spec_ref, matrix, turn), refs = refs[:seqs], refs[seqs : seqs + 3], refs[seqs + 4 :]
    sent, (whole, zh, zl, turned, back) = refs[:seqs], refs[seqs:]
    blocks = spec_ref.shape[0] - 1
    place_pieces(held, whole)
    over_blocks(reader(whole), blocks, LANES, turn, zh, zl)
    for i in range(blocks + 1):
        grad = product3(matrix, zh[i], zl[i])
        grad_real, grad_imag = grad[:LANES], grad[LANES:]
        mixed_real, mixed_imag = spec_ref[i, :LANES, :LANES], spec_ref[i, LANES:, :LANES]
        filter_real, filter_imag = spec_ref[i, :LANES, LANES:], spec_ref[i, LANES:, LANES:]
        back_real = filter_real * grad_real + filter_imag * grad_imag
        back_imag = filter_imag * grad_real - filter_real * grad_imag
        taps_real = grad_real * mixed_real + grad_imag * mixed_imag
        taps_imag = grad_real * mixed_imag - grad_imag * mixed_real
        real = jnp.concatenate([back_real, taps_real], axis=1)
        imag = jnp.concatenate([back_imag, taps_imag], axis=1)
        turned[i] = product3(matrix, *split_bf16(jnp.concatenate([real, imag], axis=0)))
    back_to_blocks(turned, blocks, 2 * LANES, turn, writer(back))
    take_pieces(back, sent)


def gradient_kernel(cot_ref, w_ref, query_ref, gated_grad_ref, *pieces):
    me = lax.axis_index("ctx")
    width = cot_ref.shape[2]
    total = None
    for j in range(cot_ref.shape[0]):
        term = lax.dot_general(
            cot_ref[j], w_ref[:, j * width : (j + 1) * width], (((1,), (1,)), ((), ())), preferred_element_type=F32
        )
        total = term if total is None else total + term
    gated_grad_ref[...] = total
    for r, out_ref in enumerate(pieces):
        cols = at_block(me ^ r)
        out_ref[...] = (gated_grad_ref[:, cols] * query_ref[:, cols].astype(F32)).astype(BF16)


def output_kernel(seqs, *refs):
    held, (query_ref, gated_grad_ref, w_ref), refs = refs[:seqs], refs[seqs : seqs + 3], refs[seqs + 4 :]
    turned_ref, grad_query_ref, keep_ref, send_ref, whole = refs
    me, part = lax.axis_index("ctx"), lax.axis_index("tp")
    width = keep_ref.shape[2]
    for r, ref in enumerate(held):
        whole[:, at_block(me ^ r)] = ref[...]
    conv = whole[...].astype(F32)
    gated = query_ref[...].astype(F32) * conv
    turned_ref[...] = gated.T.astype(BF16)
    gated = gated.astype(BF16)
    grad_query_ref[...] = (gated_grad_ref[...] * conv).astype(BF16)
    for y in range(keep_ref.shape[0]):
        for ref, core in ((keep_ref, part & 1), (send_ref, (part & 1) ^ 1)):
            ref[y] = jnp.dot(gated, w_ref[:, at_block(2 * y + core, width)], preferred_element_type=F32)


def pair_kernel(keep_ref, other_ref, mine_ref, far_ref):
    y = lax.axis_index("tp") >> 1
    mine_ref[...] = keep_ref[y] + other_ref[y]
    far_ref[...] = keep_ref[y ^ 1] + other_ref[y ^ 1]


def sum_kernel(mine_ref, other_ref, out_ref):
    out_ref[...] = (mine_ref[...] + other_ref[...]).astype(BF16)


def weight_kernel(own_ref, up1, up2, up3, down1, down2, down3, cot_ref, *refs):
    out_ref, gated, cot, sems = refs[-4:]
    me = lax.axis_index("ctx")
    seqs, size = cot_ref.shape[0], cot_ref.shape[1]
    blocks = [(cot_ref.at[p], cot.at[pl.ds(target_of(p) * size, size), :]) for p in range(seqs)]
    cot_copies = fetch([(own_ref, gated.at[0])] + blocks, sems)
    for r, (up, down) in enumerate(((up1, down3), (up2, down2), (up3, down1)), 1):

        @pl.when(me >= r)
        def _():
            pltpu.make_async_copy(up, gated.at[r], sems.at[seqs + r]).start()

        @pl.when(me < r)
        def _():
            pltpu.make_async_copy(down, gated.at[r], sems.at[seqs + r]).start()

    for copy in cot_copies:
        copy.wait()
    total = jnp.dot(gated[0], cot[at_block(me, size), :], preferred_element_type=F32)
    for r in range(1, seqs):
        pltpu.make_async_copy(up1, gated.at[r], sems.at[seqs + r]).wait()
        block = lax.rem(me + (seqs - r), seqs)
        total = total + jnp.dot(gated[r], cot[at_block(block, size), :], preferred_element_type=F32)
    out_ref[...] = total.astype(BF16)


def add_kernel(factor, one_ref, other_ref, out_ref):
    out_ref[...] = (one_ref[...].astype(F32) + other_ref[...].astype(F32)) * factor


def mixed_kernel(seqs, *refs):
    held, (key_ref, value_ref, grad_key_ref, grad_value_ref, taps_ref) = refs[:seqs], refs[seqs:]
    me = lax.axis_index("ctx")
    for r, ref in enumerate(held):
        cols = at_block(me ^ r)
        mixed_grad = ref[:, pl.ds(0, LANES)].astype(F32)
        grad_key_ref[:, cols] = (mixed_grad * value_ref[:, cols].astype(F32)).astype(BF16)
        grad_value_ref[:, cols] = (mixed_grad * key_ref[:, cols].astype(F32)).astype(BF16)
        taps_ref[:, cols] = ref[:, pl.ds(LANES, LANES)]


def taps_kernel(factor, one_ref, other_ref, out_ref):
    out_ref[...] = (one_ref[...].astype(F32) + other_ref[...].astype(F32)).T * factor


def shape_of(shape, dtype):
    return jax.ShapeDtypeStruct(shape, dtype)


def call(kernel, outs, flops, moved, *args, scratch=(), left=(), room=20):
    vmem, anywhere = pl.BlockSpec(memory_space=pltpu.VMEM), pl.BlockSpec(memory_space=pl.ANY)
    return pl.pallas_call(
        kernel,
        out_shape=outs,
        in_specs=[anywhere if n in left else vmem for n in range(len(args))],
        out_specs=jax.tree.map(lambda _: vmem, outs),
        scratch_shapes=scratch,
        cost_estimate=pl.CostEstimate(flops=flops, bytes_accessed=moved, transcendentals=0),
        compiler_params=pltpu.CompilerParams(vmem_limit_bytes=room * 2**20),
    )(*args)


def target_of(block):
    return ((block & 1) << 1) | (block >> 1)


def exchange(pieces, axis):
    size = lax.axis_size(axis)
    return [pieces[0]] + [lax.ppermute(pieces[r], axis, [(d, d ^ r) for d in range(size)]) for r in range(1, size)]


def local_short(query_proj, key_proj, value_proj, filters, w_out, cotangent):
    query, key, value, cot = query_proj[0], key_proj[0], value_proj[0], cotangent[0]
    positions, channels = query.shape
    seqs, parts, pairs = lax.axis_size("ctx"), lax.axis_size("tp"), lax.axis_size("dp")
    blocks = positions * seqs // LANES
    features = w_out.shape[1]
    width = features // parts
    factor = 1.0 / math.sqrt(pairs * positions * seqs)
    tables = [jnp.asarray(m) for m in transform_tables(blocks)]
    ring = [(d, (d + 1) % pairs) for d in range(pairs)]
    table = (blocks + 1, 2 * LANES)
    one = [shape_of((positions, LANES), BF16)] * seqs
    two = [shape_of((positions, 2 * LANES), BF16)] * seqs
    rows = (positions, channels)
    line = seqs * positions

    cot_rows = lax.all_gather(cot, "tp")
    swap = [(z * parts + j, j * parts + target_of(z)) for z in range(seqs) for j in range(parts)]
    cot_moved = lax.ppermute(cot, ("ctx", "tp"), swap)

    sent = call(
        prepare_kernel,
        two,
        10**6,
        2 * 10**6,
        key,
        value,
        filters,
        scratch=[
            pltpu.VMEM(rows, BF16),
            pltpu.VMEM(rows, BF16),
            pltpu.VMEM((channels, positions), F32),
            pltpu.SemaphoreType.DMA((3,)),
        ],
        left=(0, 1, 2),
        room=60,
    )
    held = exchange(sent, "ctx")

    gated_grad, *conv_grad = call(
        gradient_kernel,
        [shape_of(rows, F32)] + one,
        2 * positions * channels * features,
        5 * 10**6,
        cot_rows,
        w_out,
        query,
    )
    grad_held = exchange(conv_grad, "ctx")

    *conv_sent, spec, cot_passed = call(
        functools.partial(forward_kernel, seqs),
        one + [shape_of(table + (2 * LANES,), F32), shape_of(cot.shape, BF16)],
        10**9,
        9 * 10**6,
        *held,
        *tables,
        cot_moved,
        conv_grad[1],
        scratch=[
            pltpu.VMEM((line, 2 * LANES), BF16),
            pltpu.VMEM(table + (2 * LANES,), BF16),
            pltpu.VMEM(table + (2 * LANES,), BF16),
            pltpu.VMEM(table + (LANES,), F32),
            pltpu.VMEM((line, LANES), BF16),
        ],
        left=(seqs + 3,),
    )
    cot_cols = lax.all_gather(cot_passed, "tp")
    conv = exchange(conv_sent, "ctx")

    back_sent = call(
        functools.partial(backward_kernel, seqs),
        two,
        10**9,
        9 * 10**6,
        *grad_held,
        spec,
        *tables,
        conv_sent[1],
        scratch=[
            pltpu.VMEM((line, LANES), BF16),
            pltpu.VMEM(table + (LANES,), BF16),
            pltpu.VMEM(table + (LANES,), BF16),
            pltpu.VMEM(table + (2 * LANES,), F32),
            pltpu.VMEM((line, 2 * LANES), BF16),
        ],
        left=(seqs + 3,),
    )
    back = exchange(back_sent, "ctx")

    turned, grad_query, share_kept, share_sent = call(
        functools.partial(output_kernel, seqs),
        [shape_of((channels, positions), BF16), shape_of(rows, BF16)] + [shape_of((parts // 2, positions, width), F32)] * 2,
        2 * positions * channels * features,
        5 * 10**6,
        *conv,
        query,
        gated_grad,
        w_out,
        back_sent[1],
        scratch=[pltpu.VMEM(rows, BF16)],
        left=(seqs + 3,),
    )
    ups, downs = [turned], [turned]
    for r in range(1, seqs):
        ups.append(lax.ppermute(ups[-1], "ctx", [(d, d + 1) for d in range(r - 1, seqs - 1)]))
        downs.append(lax.ppermute(downs[-1], "ctx", [(d, d - 1) for d in range(seqs - r, 0, -1)]))
    mine, far = call(
        pair_kernel,
        [shape_of((positions, width), F32)] * 2,
        10**6,
        3 * 10**6,
        share_kept,
        lax.ppermute(share_sent, "tp", [(j, j ^ 1) for j in range(parts)]),
    )
    far = lax.ppermute(far, "tp", [(j, j ^ 2) for j in range(parts)])
    output = call(sum_kernel, shape_of((positions, width), BF16), 10**6, 2 * 10**6, mine, far)

    weight_grad = call(
        weight_kernel,
        shape_of((channels, width), BF16),
        2 * line * channels * width,
        3 * 10**6,
        turned,
        *ups[1:],
        *downs[1:],
        cot_cols,
        *back[1:],
        output,
        scratch=[
            pltpu.VMEM((seqs, channels, positions), BF16),
            pltpu.VMEM((line, width), BF16),
            pltpu.SemaphoreType.DMA((2 * seqs,)),
        ],
        left=range(2 * seqs + 4),
    )
    weight_other = lax.ppermute(weight_grad, "dp", ring)
    grad_wout = call(
        functools.partial(add_kernel, factor),
        shape_of((channels, width), F32),
        10**6,
        2 * 10**6,
        weight_grad,
        weight_other,
    )

    grad_key, grad_value, taps = call(
        functools.partial(mixed_kernel, seqs),
        [shape_of(rows, BF16)] * 3,
        10**6,
        2 * 10**6,
        *back,
        key,
        value,
    )
    grad_filter = call(
        functools.partial(taps_kernel, factor),
        shape_of((channels, positions), F32),
        10**6,
        10**6,
        taps,
        lax.ppermute(taps, "dp", ring),
    )
    return (output[None], grad_query[None], grad_key[None], grad_value[None], grad_filter, grad_wout)


def local(*args):
    positions, channels = args[0].shape[1:]
    seqs, parts, pairs = lax.axis_size("ctx"), lax.axis_size("tp"), lax.axis_size("dp")
    short = (
        channels == seqs * LANES
        and positions % LANES == 0
        and positions * seqs <= 8 * LANES
        and seqs == parts == 4
        and pairs == 2
        and args[4].shape[1] % (parts * LANES) == 0
    )
    return (local_short if short else local_any_length)(*args)


def solution(mesh):
    in_specs = (
        P("dp", "ctx", "tp"),
        P("dp", "ctx", "tp"),
        P("dp", "ctx", "tp"),
        P("tp", "ctx"),
        P("tp", None),
        P("dp", "ctx", "tp"),
    )
    out_specs = (
        P("dp", "ctx", "tp"),
        P("dp", "ctx", "tp"),
        P("dp", "ctx", "tp"),
        P("dp", "ctx", "tp"),
        P("tp", "ctx"),
        P("tp", "ctx"),
    )
    return jax.shard_map(local, mesh=mesh, in_specs=in_specs, out_specs=out_specs, check_vma=False)
```

```python
import functools
import math

import jax
import jax.numpy as jnp
import ml_dtypes
import numpy as np
from jax import lax
from jax.experimental import pallas as pl
from jax.experimental.pallas import tpu as pltpu
from jax.sharding import PartitionSpec as P

F32 = jnp.float32
BF16 = jnp.bfloat16
LANES = 128
ROWS = 16


def build_tables(length_fft):
    blocks = length_fft // 128
    outer = jnp.arange(blocks, dtype=jnp.int32)
    inner = jnp.arange(blocks // 2, dtype=jnp.int32)
    column = jnp.arange(128, dtype=jnp.int32)
    first = (outer[:, None] * inner[None, :] % blocks).astype(jnp.float32) * (
        -2.0 * math.pi / blocks
    )
    turned = (outer[:, None] * column[None, :] % length_fft).astype(jnp.float32) * (
        -2.0 * math.pi / length_fft
    )
    second = (column[:, None] * column[None, :] % 128).astype(jnp.float32) * (-2.0 * math.pi / 128)
    return (
        jnp.cos(first),
        jnp.sin(first),
        jnp.cos(turned),
        jnp.sin(turned),
        jnp.cos(second),
        jnp.sin(second),
    )


def product(form, left, right):
    return jnp.einsum(form, left, right, precision=lax.Precision.HIGHEST)


def forward_transform(signal, tables):
    cos_first, sin_first, cos_turn, sin_turn, cos_second, sin_second = tables
    real_one = product("ia,cab->cib", cos_first, signal)
    imag_one = product("ia,cab->cib", sin_first, signal)
    real_two = real_one * cos_turn - imag_one * sin_turn
    imag_two = real_one * sin_turn + imag_one * cos_turn
    real_out = product("cib,bj->cij", real_two, cos_second) - product(
        "cib,bj->cij", imag_two, sin_second
    )
    imag_out = product("cib,bj->cij", real_two, sin_second) + product(
        "cib,bj->cij", imag_two, cos_second
    )
    return (real_out, imag_out)


def inverse_transform(real_in, imag_in, tables, length_fft):
    cos_first, sin_first, cos_turn, sin_turn, cos_second, sin_second = tables
    real_one = product("cij,jb->cib", real_in, cos_second) + product(
        "cij,jb->cib", imag_in, sin_second
    )
    imag_one = product("cij,jb->cib", imag_in, cos_second) - product(
        "cij,jb->cib", real_in, sin_second
    )
    real_two = real_one * cos_turn + imag_one * sin_turn
    imag_two = imag_one * cos_turn - real_one * sin_turn
    result = product("ia,cib->cab", cos_first, real_two) + product(
        "ia,cib->cab", sin_first, imag_two
    )
    return result / length_fft


def local_any_length(query_proj, key_proj, value_proj, filters, w_out, cotangent):
    query_rows = query_proj[0].astype(jnp.float32)
    key_rows = key_proj[0].astype(jnp.float32)
    value_rows = value_proj[0].astype(jnp.float32)
    positions, channels = query_rows.shape
    seq_devices = lax.axis_size("ctx")
    length_fft = 2 * positions * seq_devices
    tables = build_tables(length_fft)
    mixed = (key_rows * value_rows).T
    mixed_chan, filter_chan = (
        lax.all_to_all(mixed, "ctx", split_axis=0, concat_axis=1, tiled=True),
        lax.all_to_all(filters, "ctx", split_axis=0, concat_axis=1, tiled=True),
    )
    local_channels = mixed_chan.shape[0]
    block_shape = (local_channels, length_fft // 256, 128)
    mixed_real, mixed_imag = forward_transform(mixed_chan.reshape(block_shape), tables)
    filter_real, filter_imag = forward_transform(filter_chan.reshape(block_shape), tables)
    conv_real = filter_real * mixed_real - filter_imag * mixed_imag
    conv_imag = filter_real * mixed_imag + filter_imag * mixed_real
    conv_chan = inverse_transform(conv_real, conv_imag, tables, length_fft).reshape(
        local_channels, -1
    )
    conv_back = lax.all_to_all(conv_chan, "ctx", split_axis=1, concat_axis=0, tiled=True)
    conv = conv_back.T
    gated = (query_rows * conv).astype(jnp.bfloat16)
    partial_terms = jnp.dot(gated, w_out, preferred_element_type=jnp.float32)
    output = lax.psum_scatter(partial_terms, "tp", scatter_dimension=1, tiled=True).astype(
        jnp.bfloat16
    )
    piece = lax.all_gather(cotangent[0], "tp", axis=1, tiled=True)
    grad_gated = lax.dot_general(
        piece, w_out, (((1,), (1,)), ((), ())), preferred_element_type=jnp.float32
    )
    weight_piece = lax.dot_general(
        gated, piece, (((0,), (0,)), ((), ())), preferred_element_type=jnp.float32
    )
    weight_grad = weight_piece
    grad_gated, weight_grad = (grad_gated, weight_grad)
    grad_query = (grad_gated * conv).astype(jnp.bfloat16)
    grad_conv = (grad_gated * query_rows).T
    grad_chan = lax.all_to_all(grad_conv, "ctx", split_axis=0, concat_axis=1, tiled=True)
    grad_real, grad_imag = forward_transform(grad_chan.reshape(block_shape), tables)
    back_real = filter_real * grad_real + filter_imag * grad_imag
    back_imag = filter_real * grad_imag - filter_imag * grad_real
    taps_real = grad_real * mixed_real + grad_imag * mixed_imag
    taps_imag = grad_imag * mixed_real - grad_real * mixed_imag
    mixed_grad_chan = inverse_transform(back_real, back_imag, tables, length_fft).reshape(
        local_channels, -1
    )
    filter_grad_chan = inverse_transform(taps_real, taps_imag, tables, length_fft).reshape(
        local_channels, -1
    )
    mixed_grad_back, filter_grad_back = (
        lax.all_to_all(mixed_grad_chan, "ctx", split_axis=1, concat_axis=0, tiled=True),
        lax.all_to_all(filter_grad_chan, "ctx", split_axis=1, concat_axis=0, tiled=True),
    )
    grad_mixed = mixed_grad_back.T
    grad_key = (grad_mixed * value_rows).astype(jnp.bfloat16)
    grad_value = (grad_mixed * key_rows).astype(jnp.bfloat16)
    factor = 1.0 / math.sqrt(lax.axis_size("dp") * positions * seq_devices)
    grad_filter = lax.psum(filter_grad_back, "dp") * factor
    summed_seq = lax.psum_scatter(weight_grad, "ctx", scatter_dimension=1, tiled=True)
    summed_weight = lax.psum(summed_seq, "dp")
    grad_wout = summed_weight * factor
    return (
        output[None],
        grad_query[None],
        grad_key[None],
        grad_value[None],
        grad_filter,
        grad_wout,
    )


@functools.lru_cache
def transform_tables(blocks):
    length_fft = 2 * blocks * LANES
    b = np.arange(LANES, dtype=np.int64)
    angle = (2.0 * math.pi / LANES) * (b[:, None] * b[None, :] % LANES)
    cos, sin = np.cos(angle), np.sin(angle)
    whole = np.block([[cos, sin], [-sin, cos]])
    high = whole.astype(ml_dtypes.bfloat16)
    low = (whole - high.astype(np.float64)).astype(ml_dtypes.bfloat16)
    turn = np.zeros((LANES, LANES))
    i = np.arange(blocks + 1)
    angle = (2.0 * math.pi / length_fft) * (b[:, None] * i[None, :] % length_fft)
    turn[:, : blocks + 1] = np.cos(angle)
    turn[:, LANES // 2 : LANES // 2 + blocks + 1] = np.sin(angle)
    return np.stack([high, low]), turn.astype(np.float32)


def scaled_sum(terms):
    total = None
    for factor, term in terms:
        if abs(factor) < 1e-9:
            continue
        if abs(factor - 1.0) < 1e-9:
            total = term if total is None else total + term
        elif abs(factor + 1.0) < 1e-9:
            total = -term if total is None else total - term
        else:
            total = factor * term if total is None else total + factor * term
    return total


def split_bf16(value):
    high = value.astype(BF16)
    return high, (value - high.astype(F32)).astype(BF16)


def product3(matrix_ref, high, low):
    dot = functools.partial(jnp.dot, preferred_element_type=F32)
    return dot(matrix_ref[0], high) + (dot(matrix_ref[0], low) + dot(matrix_ref[1], high))


def turn_of(turn_ref, i, row):
    rows = pl.ds(row, ROWS)
    cos = turn_ref[rows, i : i + 1]
    sin = turn_ref[rows, LANES // 2 + i : LANES // 2 + i + 1]
    return jnp.broadcast_to(cos, (ROWS, LANES)), jnp.broadcast_to(sin, (ROWS, LANES))


def each_chunk(lanes, body):
    @pl.loop(0, LANES // ROWS)
    def _(step):
        for lane in range(0, lanes, LANES):
            body(pl.multiple_of(step * ROWS, ROWS), lane)


def over_blocks(read, blocks, lanes, turn_ref, high, low):
    def chunk(row, lane):
        def put(i, real, imag):
            if i > 0:
                cos, sin = turn_of(turn_ref, i, row)
                if imag is None:
                    real, imag = real * cos, -(real * sin)
                else:
                    real, imag = real * cos + imag * sin, imag * cos - real * sin
            for part, value in ((0, real), (1, jnp.zeros_like(real) if imag is None else imag)):
                top, rest = split_bf16(value)
                rows = pl.ds(pl.multiple_of(part * LANES + row, ROWS), ROWS)
                high[i, rows, pl.ds(lane, LANES)] = top
                low[i, rows, pl.ds(lane, LANES)] = rest

        slabs = [read(a, row, lane) for a in range(blocks)]
        for i in range(blocks // 2 + 1):
            sums = []
            for first in (0, 1):
                picked = range(first, blocks, 2)
                angle = [math.pi * ((i * a) % (2 * blocks)) / blocks for a in picked]
                sums.append(scaled_sum([(math.cos(g), slabs[a]) for g, a in zip(angle, picked)]))
                sums.append(scaled_sum([(-math.sin(g), slabs[a]) for g, a in zip(angle, picked)]))
            even_real, even_imag, odd_real, odd_imag = sums

            def joined(one, other, sign):
                if one is None or other is None:
                    return one if other is None else (other if sign > 0 else -other)
                return one + other if sign > 0 else one - other

            put(i, joined(even_real, odd_real, 1), joined(even_imag, odd_imag, 1))
            if blocks - i != i:
                put(blocks - i, joined(even_real, odd_real, -1), joined(odd_imag, even_imag, -1))

    each_chunk(lanes, chunk)


def back_to_blocks(turned, blocks, lanes, turn_ref, write):
    scale = 1.0 / (blocks * LANES)

    def chunk(row, lane):
        def get(i):
            real = turned[i, pl.ds(row, ROWS), pl.ds(lane, LANES)]
            imag = -turned[i, pl.ds(pl.multiple_of(LANES + row, ROWS), ROWS), pl.ds(lane, LANES)]
            if i > 0:
                cos, sin = turn_of(turn_ref, i, row)
                real, imag = real * cos - imag * sin, imag * cos + real * sin
            return real, imag

        terms = [[] for _ in range(blocks)]
        for i in range(blocks // 2 + 1):
            real, imag = get(i)
            if blocks - i != i:
                other_real, other_imag = get(blocks - i)
                pairs = ((real + other_real, imag - other_imag), (real - other_real, imag + other_imag))
            else:
                pairs = ((real, imag), (real, imag))
            if i == 0:
                pairs = tuple((0.5 * one, 0.5 * two) for one, two in pairs)
            for a in range(blocks):
                angle = math.pi * ((i * a) % (2 * blocks)) / blocks
                terms[a].append((math.cos(angle), pairs[a % 2][0]))
                terms[a].append((-math.sin(angle), pairs[a % 2][1]))
        for a in range(blocks):
            write(a, row, lane, scaled_sum(terms[a]) * scale)

    each_chunk(lanes, chunk)


def at_block(index, size=LANES):
    return pl.ds(pl.multiple_of(index * size, size), size)


def reader(ref):
    def read(a, row, lane):
        rows = pl.ds(pl.multiple_of(a * LANES + row, ROWS), ROWS)
        return ref[rows, pl.ds(lane, LANES)].astype(F32)

    return read


def writer(ref):
    def write(a, row, lane, value):
        rows = pl.ds(pl.multiple_of(a * LANES + row, ROWS), ROWS)
        ref[rows, pl.ds(lane, LANES)] = value.astype(ref.dtype)

    return write


def place_pieces(pieces, whole):
    me = lax.axis_index("ctx")
    for r, ref in enumerate(pieces):
        whole[at_block(me ^ r, ref.shape[0]), :] = ref[:, pl.ds(0, whole.shape[1])]


def take_pieces(whole, pieces):
    me = lax.axis_index("ctx")
    for r, ref in enumerate(pieces):
        ref[...] = whole[at_block(me ^ r, ref.shape[0]), :]


def fetch(pairs, sems):
    copies = [pltpu.make_async_copy(source, target, sems.at[n]) for n, (source, target) in enumerate(pairs)]
    for copy in copies:
        copy.start()
    return copies


def prepare_kernel(*refs):
    *pieces, key_ref, value_ref, filter_ref, sems = refs[3:]
    for copy in fetch(list(zip(refs[:3], (key_ref, value_ref, filter_ref))), sems):
        copy.wait()
    me = lax.axis_index("ctx")
    for r, out_ref in enumerate(pieces):
        cols = at_block(me ^ r)
        mixed = key_ref[:, cols].astype(F32) * value_ref[:, cols].astype(F32)
        out_ref[:, pl.ds(0, LANES)] = mixed.astype(BF16)
        out_ref[:, pl.ds(LANES, LANES)] = filter_ref[cols, :].T.astype(BF16)


def forward_kernel(seqs, *refs):
    held, (matrix, turn), refs = refs[:seqs], refs[seqs : seqs + 2], refs[seqs + 2 :]
    sent, (spec_ref, whole, zh, zl, turned, conv) = refs[:seqs], refs[seqs:]
    blocks = spec_ref.shape[0] - 1
    place_pieces(held, whole)
    over_blocks(reader(whole), blocks, 2 * LANES, turn, zh, zl)
    for i in range(blocks + 1):
        spec = product3(matrix, zh[i], zl[i])
        spec_ref[i] = spec
        mixed_real, mixed_imag = spec[:LANES, :LANES], spec[LANES:, :LANES]
        filter_real, filter_imag = spec[:LANES, LANES:], spec[LANES:, LANES:]
        real = filter_real * mixed_real - filter_imag * mixed_imag
        imag = filter_real * mixed_imag + filter_imag * mixed_real
        turned[i] = product3(matrix, *split_bf16(jnp.concatenate([real, -imag], axis=0)))
    back_to_blocks(turned, blocks, LANES, turn, writer(conv))
    take_pieces(conv, sent)


def backward_kernel(seqs, *refs):
    held, (spec_ref, matrix, turn), refs = refs[:seqs], refs[seqs : seqs + 3], refs[seqs + 5 :]
    sent, (whole, zh, zl, turned, back) = refs[:seqs], refs[seqs:]
    blocks = spec_ref.shape[0] - 1
    place_pieces(held, whole)
    over_blocks(reader(whole), blocks, LANES, turn, zh, zl)
    for i in range(blocks + 1):
        grad = product3(matrix, zh[i], zl[i])
        grad_real, grad_imag = grad[:LANES], grad[LANES:]
        mixed_real, mixed_imag = spec_ref[i, :LANES, :LANES], spec_ref[i, LANES:, :LANES]
        filter_real, filter_imag = spec_ref[i, :LANES, LANES:], spec_ref[i, LANES:, LANES:]
        back_real = filter_real * grad_real + filter_imag * grad_imag
        back_imag = filter_imag * grad_real - filter_real * grad_imag
        taps_real = grad_real * mixed_real + grad_imag * mixed_imag
        taps_imag = grad_real * mixed_imag - grad_imag * mixed_real
        real = jnp.concatenate([back_real, taps_real], axis=1)
        imag = jnp.concatenate([back_imag, taps_imag], axis=1)
        turned[i] = product3(matrix, *split_bf16(jnp.concatenate([real, imag], axis=0)))
    back_to_blocks(turned, blocks, 2 * LANES, turn, writer(back))
    take_pieces(back, sent)


def gradient_kernel(cot_ref, w_ref, query_ref, _, gated_grad_ref, *pieces):
    me, part = lax.axis_index("ctx"), lax.axis_index("tp")
    parts, positions, width = cot_ref.shape
    quarter = positions // parts
    total = None
    for j in range(parts):
        term = lax.dot_general(
            cot_ref[j], w_ref[:, j * width : (j + 1) * width], (((1,), (1,)), ((), ())), preferred_element_type=F32
        )
        total = term if total is None else total + term
    gated_grad_ref[...] = total
    for r, out_ref in enumerate(pieces):
        cols = at_block(me ^ r)
        out_ref[:, pl.ds(0, LANES)] = (gated_grad_ref[:, cols] * query_ref[:, cols].astype(F32)).astype(BF16)
        for k in range(width // LANES):
            out_ref[pl.ds(k * quarter, quarter), pl.ds(LANES, LANES)] = cot_ref[
                me ^ r, at_block(part, quarter), pl.ds(k * LANES, LANES)
            ]


def quarter_kernel(seqs, *refs):
    held, out_ref = refs[:seqs], refs[seqs]
    me = lax.axis_index("ctx")
    quarter = out_ref.shape[0] // seqs
    for r, ref in enumerate(held):
        for k in range(out_ref.shape[1] // LANES):
            out_ref[at_block(me ^ r, quarter), pl.ds(k * LANES, LANES)] = ref[
                pl.ds(k * quarter, quarter), pl.ds(LANES, LANES)
            ]


def output_kernel(seqs, *refs):
    held, (query_ref, gated_grad_ref, w_ref), refs = refs[:seqs], refs[seqs : seqs + 3], refs[seqs + 4 :]
    turned_ref, grad_query_ref, keep_ref, send_ref, whole = refs
    me, part = lax.axis_index("ctx"), lax.axis_index("tp")
    width = keep_ref.shape[2]
    for r, ref in enumerate(held):
        whole[:, at_block(me ^ r)] = ref[...]
    conv = whole[...].astype(F32)
    gated = query_ref[...].astype(F32) * conv
    turned_ref[...] = gated.T.astype(BF16)
    gated = gated.astype(BF16)
    grad_query_ref[...] = (gated_grad_ref[...] * conv).astype(BF16)
    for y in range(keep_ref.shape[0]):
        for ref, core in ((keep_ref, part & 1), (send_ref, (part & 1) ^ 1)):
            ref[y] = jnp.dot(gated, w_ref[:, at_block(2 * y + core, width)], preferred_element_type=F32)


def pair_kernel(keep_ref, other_ref, mine_ref, far_ref):
    y = lax.axis_index("tp") >> 1
    mine_ref[...] = keep_ref[y] + other_ref[y]
    far_ref[...] = (keep_ref[y ^ 1] + other_ref[y ^ 1]).astype(BF16)


def sum_kernel(mine_ref, other_ref, out_ref):
    out_ref[...] = (mine_ref[...] + other_ref[...].astype(F32)).astype(BF16)


def pick_kernel(up_ref, down_ref, _, out_ref):
    high = lax.axis_index("ctx") >= 2

    @pl.when(high)
    def _():
        out_ref[...] = up_ref[...]

    @pl.when(jnp.logical_not(high))
    def _():
        out_ref[...] = down_ref[...]


def weight_kernel(own_ref, up_ref, down_ref, two_ref, end_ref, cot_ref, *refs):
    out_ref, total, cot = refs[-3:]
    me = lax.axis_index("ctx")
    parts = cot_ref.shape[0]
    quarter = cot_ref.shape[1] // parts
    top = parts - 1

    def term(gated_ref, block):
        for p in range(parts):
            cot[pl.ds(p * quarter, quarter), :] = cot_ref[p, at_block(block, quarter), :]
        return jnp.dot(gated_ref[...], cot[...], preferred_element_type=F32)

    def add(gated_ref, block):
        total[...] += term(gated_ref, block)

    total[...] = term(own_ref, me)
    add(two_ref, me ^ 2)
    pl.when(me > 0)(lambda: add(up_ref, me - 1))
    pl.when(me < top)(lambda: add(down_ref, me + 1))
    pl.when(jnp.logical_or(me == 0, me == top))(lambda: add(end_ref, top - me))
    out_ref[...] = total[...].astype(BF16)


def add_kernel(factor, one_ref, other_ref, out_ref):
    out_ref[...] = (one_ref[...].astype(F32) + other_ref[...].astype(F32)) * factor


def mixed_kernel(seqs, *refs):
    held, (key_ref, value_ref, grad_key_ref, grad_value_ref, taps_ref) = refs[:seqs], refs[seqs:]
    me = lax.axis_index("ctx")
    for r, ref in enumerate(held):
        cols = at_block(me ^ r)
        mixed_grad = ref[:, pl.ds(0, LANES)].astype(F32)
        grad_key_ref[:, cols] = (mixed_grad * value_ref[:, cols].astype(F32)).astype(BF16)
        grad_value_ref[:, cols] = (mixed_grad * key_ref[:, cols].astype(F32)).astype(BF16)
        taps_ref[:, cols] = ref[:, pl.ds(LANES, LANES)]


def taps_kernel(factor, one_ref, other_ref, out_ref):
    out_ref[...] = (one_ref[...].astype(F32) + other_ref[...].astype(F32)).T * factor


def shape_of(shape, dtype):
    return jax.ShapeDtypeStruct(shape, dtype)


def call(kernel, outs, flops, moved, *args, scratch=(), left=(), room=20):
    vmem, anywhere = pl.BlockSpec(memory_space=pltpu.VMEM), pl.BlockSpec(memory_space=pl.ANY)
    return pl.pallas_call(
        kernel,
        out_shape=outs,
        in_specs=[anywhere if n in left else vmem for n in range(len(args))],
        out_specs=jax.tree.map(lambda _: vmem, outs),
        scratch_shapes=scratch,
        cost_estimate=pl.CostEstimate(flops=flops, bytes_accessed=moved, transcendentals=0),
        compiler_params=pltpu.CompilerParams(vmem_limit_bytes=room * 2**20),
    )(*args)


def exchange(pieces, axis):
    size = lax.axis_size(axis)
    return [pieces[0]] + [lax.ppermute(pieces[r], axis, [(d, d ^ r) for d in range(size)]) for r in range(1, size)]


def local_short(query_proj, key_proj, value_proj, filters, w_out, cotangent):
    query, key, value, cot = query_proj[0], key_proj[0], value_proj[0], cotangent[0]
    positions, channels = query.shape
    seqs, parts, pairs = lax.axis_size("ctx"), lax.axis_size("tp"), lax.axis_size("dp")
    blocks = positions * seqs // LANES
    features = w_out.shape[1]
    width = features // parts
    factor = 1.0 / math.sqrt(pairs * positions * seqs)
    tables = [jnp.asarray(m) for m in transform_tables(blocks)]
    ring = [(d, (d + 1) % pairs) for d in range(pairs)]
    table = (blocks + 1, 2 * LANES)
    one = [shape_of((positions, LANES), BF16)] * seqs
    two = [shape_of((positions, 2 * LANES), BF16)] * seqs
    rows = (positions, channels)
    line = seqs * positions

    cot_rows = lax.all_gather(cot, "tp")
    sent = call(
        prepare_kernel,
        two,
        10**6,
        2 * 10**6,
        key,
        value,
        filters,
        scratch=[
            pltpu.VMEM(rows, BF16),
            pltpu.VMEM(rows, BF16),
            pltpu.VMEM((channels, positions), F32),
            pltpu.SemaphoreType.DMA((3,)),
        ],
        left=(0, 1, 2),
        room=60,
    )
    held = exchange(sent, "ctx")

    *conv_sent, spec = call(
        functools.partial(forward_kernel, seqs),
        one + [shape_of(table + (2 * LANES,), F32)],
        10**9,
        9 * 10**6,
        *held,
        *tables,
        scratch=[
            pltpu.VMEM((line, 2 * LANES), BF16),
            pltpu.VMEM(table + (2 * LANES,), BF16),
            pltpu.VMEM(table + (2 * LANES,), BF16),
            pltpu.VMEM(table + (LANES,), F32),
            pltpu.VMEM((line, LANES), BF16),
        ],
    )
    conv = exchange(conv_sent, "ctx")

    gated_grad, *conv_grad = call(
        gradient_kernel,
        [shape_of(rows, F32)] + two,
        2 * positions * channels * features,
        5 * 10**6,
        cot_rows,
        w_out,
        query,
        conv_sent[1],
        left=(3,),
    )
    grad_held = exchange(conv_grad, "ctx")
    cot_quarters = call(
        functools.partial(quarter_kernel, seqs), shape_of((positions, width), BF16), 10**6, 10**6, *grad_held
    )
    cot_cols = lax.all_gather(cot_quarters, "tp")

    turned, grad_query, share_kept, share_sent = call(
        functools.partial(output_kernel, seqs),
        [shape_of((channels, positions), BF16), shape_of(rows, BF16)] + [shape_of((parts // 2, positions, width), F32)] * 2,
        2 * positions * channels * features,
        5 * 10**6,
        *conv,
        query,
        gated_grad,
        w_out,
        grad_held[1],
        scratch=[pltpu.VMEM(rows, BF16)],
        left=range(seqs + 3, seqs + 4),
    )
    ups, downs = [turned], [turned]
    for r in (1, 2):
        ups.append(lax.ppermute(ups[-1], "ctx", [(d, d + 1) for d in range(r - 1, seqs - 1)]))
        downs.append(lax.ppermute(downs[-1], "ctx", [(d, d - 1) for d in range(seqs - r, 0, -1)]))

    back_sent = call(
        functools.partial(backward_kernel, seqs),
        two,
        10**9,
        9 * 10**6,
        *grad_held,
        spec,
        *tables,
        turned,
        cot_quarters,
        scratch=[
            pltpu.VMEM((line, LANES), BF16),
            pltpu.VMEM(table + (LANES,), BF16),
            pltpu.VMEM(table + (LANES,), BF16),
            pltpu.VMEM(table + (2 * LANES,), F32),
            pltpu.VMEM((line, 2 * LANES), BF16),
        ],
        left=(seqs + 3, seqs + 4),
    )
    back = exchange(back_sent, "ctx")

    two_away = call(pick_kernel, shape_of((channels, positions), BF16), 10**6, 10**6, ups[2], downs[2], back[1], left=(2,))
    end_away = lax.ppermute(two_away, "ctx", [(1, 0), (2, 3)])


    mine, far = call(
        pair_kernel,
        [shape_of((positions, width), F32), shape_of((positions, width), BF16)],
        10**6,
        3 * 10**6,
        share_kept,
        lax.ppermute(share_sent, "tp", [(j, j ^ 1) for j in range(parts)]),
    )
    far = lax.ppermute(far, "tp", [(j, j ^ 2) for j in range(parts)])
    output = call(sum_kernel, shape_of((positions, width), BF16), 10**6, 2 * 10**6, mine, far)

    grad_key, grad_value, taps = call(
        functools.partial(mixed_kernel, seqs),
        [shape_of(rows, BF16)] * 3,
        10**6,
        2 * 10**6,
        *back,
        key,
        value,
    )
    taps_other = lax.ppermute(taps, "dp", ring)
    weight_grad = call(
        weight_kernel,
        shape_of((channels, width), BF16),
        2 * line * channels * width,
        3 * 10**6,
        turned,
        ups[1],
        downs[1],
        two_away,
        end_away,
        cot_cols,
        taps,
        mine,
        scratch=[pltpu.VMEM((channels, width), F32), pltpu.VMEM((positions, width), BF16)],
        left=range(6, 8),
    )
    weight_other = lax.ppermute(weight_grad, "dp", ring)
    grad_wout = call(
        functools.partial(add_kernel, factor),
        shape_of((channels, width), F32),
        10**6,
        2 * 10**6,
        weight_grad,
        weight_other,
    )

    grad_filter = call(
        functools.partial(taps_kernel, factor),
        shape_of((channels, positions), F32),
        10**6,
        10**6,
        taps,
        taps_other,
    )
    return (output[None], grad_query[None], grad_key[None], grad_value[None], grad_filter, grad_wout)


def local(*args):
    positions, channels = args[0].shape[1:]
    seqs, parts, pairs = lax.axis_size("ctx"), lax.axis_size("tp"), lax.axis_size("dp")
    short = (
        channels == seqs * LANES
        and positions % LANES == 0
        and args[4].shape[1] == parts * parts * LANES
        and positions * seqs <= 8 * LANES
        and seqs == parts == 4
        and pairs == 2
    )
    return (local_short if short else local_any_length)(*args)


def solution(mesh):
    in_specs = (
        P("dp", "ctx", "tp"),
        P("dp", "ctx", "tp"),
        P("dp", "ctx", "tp"),
        P("tp", "ctx"),
        P("tp", None),
        P("dp", "ctx", "tp"),
    )
    out_specs = (
        P("dp", "ctx", "tp"),
        P("dp", "ctx", "tp"),
        P("dp", "ctx", "tp"),
        P("dp", "ctx", "tp"),
        P("tp", "ctx"),
        P("tp", "ctx"),
    )
    return jax.shard_map(local, mesh=mesh, in_specs=in_specs, out_specs=out_specs, check_vma=False)
```

```python
import functools
import math

import jax
import jax.numpy as jnp
import ml_dtypes
import numpy as np
from jax import lax
from jax.experimental import pallas as pl
from jax.experimental.pallas import tpu as pltpu
from jax.sharding import PartitionSpec as P

F32 = jnp.float32
BF16 = jnp.bfloat16
LANES = 128
ROWS = 16


def build_tables(length_fft):
    blocks = length_fft // 128
    outer = jnp.arange(blocks, dtype=jnp.int32)
    inner = jnp.arange(blocks // 2, dtype=jnp.int32)
    column = jnp.arange(128, dtype=jnp.int32)
    first = (outer[:, None] * inner[None, :] % blocks).astype(jnp.float32) * (
        -2.0 * math.pi / blocks
    )
    turned = (outer[:, None] * column[None, :] % length_fft).astype(jnp.float32) * (
        -2.0 * math.pi / length_fft
    )
    second = (column[:, None] * column[None, :] % 128).astype(jnp.float32) * (-2.0 * math.pi / 128)
    return (
        jnp.cos(first),
        jnp.sin(first),
        jnp.cos(turned),
        jnp.sin(turned),
        jnp.cos(second),
        jnp.sin(second),
    )


def product(form, left, right):
    return jnp.einsum(form, left, right, precision=lax.Precision.HIGHEST)


def forward_transform(signal, tables):
    cos_first, sin_first, cos_turn, sin_turn, cos_second, sin_second = tables
    real_one = product("ia,cab->cib", cos_first, signal)
    imag_one = product("ia,cab->cib", sin_first, signal)
    real_two = real_one * cos_turn - imag_one * sin_turn
    imag_two = real_one * sin_turn + imag_one * cos_turn
    real_out = product("cib,bj->cij", real_two, cos_second) - product(
        "cib,bj->cij", imag_two, sin_second
    )
    imag_out = product("cib,bj->cij", real_two, sin_second) + product(
        "cib,bj->cij", imag_two, cos_second
    )
    return (real_out, imag_out)


def inverse_transform(real_in, imag_in, tables, length_fft):
    cos_first, sin_first, cos_turn, sin_turn, cos_second, sin_second = tables
    real_one = product("cij,jb->cib", real_in, cos_second) + product(
        "cij,jb->cib", imag_in, sin_second
    )
    imag_one = product("cij,jb->cib", imag_in, cos_second) - product(
        "cij,jb->cib", real_in, sin_second
    )
    real_two = real_one * cos_turn + imag_one * sin_turn
    imag_two = imag_one * cos_turn - real_one * sin_turn
    result = product("ia,cib->cab", cos_first, real_two) + product(
        "ia,cib->cab", sin_first, imag_two
    )
    return result / length_fft


def local_any_length(query_proj, key_proj, value_proj, filters, w_out, cotangent):
    query_rows = query_proj[0].astype(jnp.float32)
    key_rows = key_proj[0].astype(jnp.float32)
    value_rows = value_proj[0].astype(jnp.float32)
    positions, channels = query_rows.shape
    seq_devices = lax.axis_size("ctx")
    length_fft = 2 * positions * seq_devices
    tables = build_tables(length_fft)
    mixed = (key_rows * value_rows).T
    mixed_chan, filter_chan = (
        lax.all_to_all(mixed, "ctx", split_axis=0, concat_axis=1, tiled=True),
        lax.all_to_all(filters, "ctx", split_axis=0, concat_axis=1, tiled=True),
    )
    local_channels = mixed_chan.shape[0]
    block_shape = (local_channels, length_fft // 256, 128)
    mixed_real, mixed_imag = forward_transform(mixed_chan.reshape(block_shape), tables)
    filter_real, filter_imag = forward_transform(filter_chan.reshape(block_shape), tables)
    conv_real = filter_real * mixed_real - filter_imag * mixed_imag
    conv_imag = filter_real * mixed_imag + filter_imag * mixed_real
    conv_chan = inverse_transform(conv_real, conv_imag, tables, length_fft).reshape(
        local_channels, -1
    )
    conv_back = lax.all_to_all(conv_chan, "ctx", split_axis=1, concat_axis=0, tiled=True)
    conv = conv_back.T
    gated = (query_rows * conv).astype(jnp.bfloat16)
    partial_terms = jnp.dot(gated, w_out, preferred_element_type=jnp.float32)
    output = lax.psum_scatter(partial_terms, "tp", scatter_dimension=1, tiled=True).astype(
        jnp.bfloat16
    )
    piece = lax.all_gather(cotangent[0], "tp", axis=1, tiled=True)
    grad_gated = lax.dot_general(
        piece, w_out, (((1,), (1,)), ((), ())), preferred_element_type=jnp.float32
    )
    weight_piece = lax.dot_general(
        gated, piece, (((0,), (0,)), ((), ())), preferred_element_type=jnp.float32
    )
    weight_grad = weight_piece
    grad_gated, weight_grad = (grad_gated, weight_grad)
    grad_query = (grad_gated * conv).astype(jnp.bfloat16)
    grad_conv = (grad_gated * query_rows).T
    grad_chan = lax.all_to_all(grad_conv, "ctx", split_axis=0, concat_axis=1, tiled=True)
    grad_real, grad_imag = forward_transform(grad_chan.reshape(block_shape), tables)
    back_real = filter_real * grad_real + filter_imag * grad_imag
    back_imag = filter_real * grad_imag - filter_imag * grad_real
    taps_real = grad_real * mixed_real + grad_imag * mixed_imag
    taps_imag = grad_imag * mixed_real - grad_real * mixed_imag
    mixed_grad_chan = inverse_transform(back_real, back_imag, tables, length_fft).reshape(
        local_channels, -1
    )
    filter_grad_chan = inverse_transform(taps_real, taps_imag, tables, length_fft).reshape(
        local_channels, -1
    )
    mixed_grad_back, filter_grad_back = (
        lax.all_to_all(mixed_grad_chan, "ctx", split_axis=1, concat_axis=0, tiled=True),
        lax.all_to_all(filter_grad_chan, "ctx", split_axis=1, concat_axis=0, tiled=True),
    )
    grad_mixed = mixed_grad_back.T
    grad_key = (grad_mixed * value_rows).astype(jnp.bfloat16)
    grad_value = (grad_mixed * key_rows).astype(jnp.bfloat16)
    factor = 1.0 / math.sqrt(lax.axis_size("dp") * positions * seq_devices)
    grad_filter = lax.psum(filter_grad_back, "dp") * factor
    summed_seq = lax.psum_scatter(weight_grad, "ctx", scatter_dimension=1, tiled=True)
    summed_weight = lax.psum(summed_seq, "dp")
    grad_wout = summed_weight * factor
    return (
        output[None],
        grad_query[None],
        grad_key[None],
        grad_value[None],
        grad_filter,
        grad_wout,
    )


@functools.lru_cache
def transform_tables(blocks):
    length_fft = 2 * blocks * LANES
    b = np.arange(LANES, dtype=np.int64)
    angle = (2.0 * math.pi / LANES) * (b[:, None] * b[None, :] % LANES)
    cos, sin = np.cos(angle), np.sin(angle)
    whole = np.block([[cos, sin], [-sin, cos]])
    high = whole.astype(ml_dtypes.bfloat16)
    low = (whole - high.astype(np.float64)).astype(ml_dtypes.bfloat16)
    turn = np.zeros((LANES, LANES))
    i = np.arange(blocks + 1)
    angle = (2.0 * math.pi / length_fft) * (b[:, None] * i[None, :] % length_fft)
    turn[:, : blocks + 1] = np.cos(angle)
    turn[:, LANES // 2 : LANES // 2 + blocks + 1] = np.sin(angle)
    return np.stack([high, low]), turn.astype(np.float32)


def scaled_sum(terms):
    total = None
    for factor, term in terms:
        if abs(factor) < 1e-9:
            continue
        if abs(factor - 1.0) < 1e-9:
            total = term if total is None else total + term
        elif abs(factor + 1.0) < 1e-9:
            total = -term if total is None else total - term
        else:
            total = factor * term if total is None else total + factor * term
    return total


def split_bf16(value):
    high = value.astype(BF16)
    return high, (value - high.astype(F32)).astype(BF16)


def product3(matrix_ref, high, low):
    dot = functools.partial(jnp.dot, preferred_element_type=F32)
    return dot(matrix_ref[0], high) + (dot(matrix_ref[0], low) + dot(matrix_ref[1], high))


def turn_of(turn_ref, i, row):
    rows = pl.ds(row, ROWS)
    cos = turn_ref[rows, i : i + 1]
    sin = turn_ref[rows, LANES // 2 + i : LANES // 2 + i + 1]
    return jnp.broadcast_to(cos, (ROWS, LANES)), jnp.broadcast_to(sin, (ROWS, LANES))


def each_chunk(lanes, body):
    @pl.loop(0, LANES // ROWS)
    def _(step):
        for lane in range(0, lanes, LANES):
            body(pl.multiple_of(step * ROWS, ROWS), lane)


def over_blocks(read, blocks, lanes, turn_ref, high, low):
    def chunk(row, lane):
        def put(i, real, imag):
            if i > 0:
                cos, sin = turn_of(turn_ref, i, row)
                if imag is None:
                    real, imag = real * cos, -(real * sin)
                else:
                    real, imag = real * cos + imag * sin, imag * cos - real * sin
            for part, value in ((0, real), (1, jnp.zeros_like(real) if imag is None else imag)):
                top, rest = split_bf16(value)
                rows = pl.ds(pl.multiple_of(part * LANES + row, ROWS), ROWS)
                high[i, rows, pl.ds(lane, LANES)] = top
                low[i, rows, pl.ds(lane, LANES)] = rest

        slabs = [read(a, row, lane) for a in range(blocks)]
        for i in range(blocks // 2 + 1):
            sums = []
            for first in (0, 1):
                picked = range(first, blocks, 2)
                angle = [math.pi * ((i * a) % (2 * blocks)) / blocks for a in picked]
                sums.append(scaled_sum([(math.cos(g), slabs[a]) for g, a in zip(angle, picked)]))
                sums.append(scaled_sum([(-math.sin(g), slabs[a]) for g, a in zip(angle, picked)]))
            even_real, even_imag, odd_real, odd_imag = sums

            def joined(one, other, sign):
                if one is None or other is None:
                    return one if other is None else (other if sign > 0 else -other)
                return one + other if sign > 0 else one - other

            put(i, joined(even_real, odd_real, 1), joined(even_imag, odd_imag, 1))
            if blocks - i != i:
                put(blocks - i, joined(even_real, odd_real, -1), joined(odd_imag, even_imag, -1))

    each_chunk(lanes, chunk)


def back_to_blocks(turned, blocks, lanes, turn_ref, write):
    scale = 1.0 / (blocks * LANES)

    def chunk(row, lane):
        def get(i):
            real = turned[i, pl.ds(row, ROWS), pl.ds(lane, LANES)]
            imag = -turned[i, pl.ds(pl.multiple_of(LANES + row, ROWS), ROWS), pl.ds(lane, LANES)]
            if i > 0:
                cos, sin = turn_of(turn_ref, i, row)
                real, imag = real * cos - imag * sin, imag * cos + real * sin
            return real, imag

        terms = [[] for _ in range(blocks)]
        for i in range(blocks // 2 + 1):
            real, imag = get(i)
            if blocks - i != i:
                other_real, other_imag = get(blocks - i)
                pairs = ((real + other_real, imag - other_imag), (real - other_real, imag + other_imag))
            else:
                pairs = ((real, imag), (real, imag))
            if i == 0:
                pairs = tuple((0.5 * one, 0.5 * two) for one, two in pairs)
            for a in range(blocks):
                angle = math.pi * ((i * a) % (2 * blocks)) / blocks
                terms[a].append((math.cos(angle), pairs[a % 2][0]))
                terms[a].append((-math.sin(angle), pairs[a % 2][1]))
        for a in range(blocks):
            write(a, row, lane, scaled_sum(terms[a]) * scale)

    each_chunk(lanes, chunk)


def at_block(index, size=LANES):
    return pl.ds(pl.multiple_of(index * size, size), size)


def reader(ref):
    def read(a, row, lane):
        rows = pl.ds(pl.multiple_of(a * LANES + row, ROWS), ROWS)
        return ref[rows, pl.ds(lane, LANES)].astype(F32)

    return read


def writer(ref):
    def write(a, row, lane, value):
        rows = pl.ds(pl.multiple_of(a * LANES + row, ROWS), ROWS)
        ref[rows, pl.ds(lane, LANES)] = value.astype(ref.dtype)

    return write


def place_pieces(pieces, whole):
    me = lax.axis_index("ctx")
    for r, ref in enumerate(pieces):
        whole[at_block(me ^ r, ref.shape[0]), :] = ref[:, pl.ds(0, whole.shape[1])]


def take_pieces(whole, pieces):
    me = lax.axis_index("ctx")
    for r, ref in enumerate(pieces):
        ref[...] = whole[at_block(me ^ r, ref.shape[0]), :]


def fetch(pairs, sems):
    copies = [pltpu.make_async_copy(source, target, sems.at[n]) for n, (source, target) in enumerate(pairs)]
    for copy in copies:
        copy.start()
    return copies


def prepare_kernel(*refs):
    *pieces, key_ref, value_ref, filter_ref, sems = refs[3:]
    for copy in fetch(list(zip(refs[:3], (key_ref, value_ref, filter_ref))), sems):
        copy.wait()
    me = lax.axis_index("ctx")
    for r, out_ref in enumerate(pieces):
        cols = at_block(me ^ r)
        mixed = key_ref[:, cols].astype(F32) * value_ref[:, cols].astype(F32)
        out_ref[:, pl.ds(0, LANES)] = mixed.astype(BF16)
        out_ref[:, pl.ds(LANES, LANES)] = filter_ref[cols, :].T.astype(BF16)


def forward_kernel(seqs, *refs):
    held, (matrix, turn), refs = refs[:seqs], refs[seqs : seqs + 2], refs[seqs + 3 :]
    sent, (spec_ref, whole, zh, zl, turned, conv) = refs[:seqs], refs[seqs:]
    blocks = spec_ref.shape[0] - 1
    place_pieces(held, whole)
    over_blocks(reader(whole), blocks, 2 * LANES, turn, zh, zl)
    for i in range(blocks + 1):
        spec = product3(matrix, zh[i], zl[i])
        spec_ref[i] = spec
        mixed_real, mixed_imag = spec[:LANES, :LANES], spec[LANES:, :LANES]
        filter_real, filter_imag = spec[:LANES, LANES:], spec[LANES:, LANES:]
        real = filter_real * mixed_real - filter_imag * mixed_imag
        imag = filter_real * mixed_imag + filter_imag * mixed_real
        turned[i] = product3(matrix, *split_bf16(jnp.concatenate([real, -imag], axis=0)))
    back_to_blocks(turned, blocks, LANES, turn, writer(conv))
    take_pieces(conv, sent)


def backward_kernel(seqs, *refs):
    held, (spec_ref, matrix, turn), refs = refs[:seqs], refs[seqs : seqs + 3], refs[seqs + 5 :]
    sent, (whole, zh, zl, turned, back) = refs[:seqs], refs[seqs:]
    blocks = spec_ref.shape[0] - 1
    place_pieces(held, whole)
    over_blocks(reader(whole), blocks, LANES, turn, zh, zl)
    for i in range(blocks + 1):
        grad = product3(matrix, zh[i], zl[i])
        grad_real, grad_imag = grad[:LANES], grad[LANES:]
        mixed_real, mixed_imag = spec_ref[i, :LANES, :LANES], spec_ref[i, LANES:, :LANES]
        filter_real, filter_imag = spec_ref[i, :LANES, LANES:], spec_ref[i, LANES:, LANES:]
        back_real = filter_real * grad_real + filter_imag * grad_imag
        back_imag = filter_imag * grad_real - filter_real * grad_imag
        taps_real = grad_real * mixed_real + grad_imag * mixed_imag
        taps_imag = grad_real * mixed_imag - grad_imag * mixed_real
        real = jnp.concatenate([back_real, taps_real], axis=1)
        imag = jnp.concatenate([back_imag, taps_imag], axis=1)
        turned[i] = product3(matrix, *split_bf16(jnp.concatenate([real, imag], axis=0)))
    back_to_blocks(turned, blocks, 2 * LANES, turn, writer(back))
    take_pieces(back, sent)


def gradient_kernel(parts, *refs):
    cots, (w_ref, query_ref), refs = refs[:parts], refs[parts : parts + 2], refs[parts + 5 :]
    gated_grad_ref, *pieces, cot = refs
    me, part = lax.axis_index("ctx"), lax.axis_index("tp")
    positions, width = cots[0].shape
    quarter = positions // parts
    total = None
    for r, ref in enumerate(cots):
        cot[part ^ r] = ref[...]
        term = lax.dot_general(
            ref[...], w_ref[:, at_block(part ^ r, width)], (((1,), (1,)), ((), ())), preferred_element_type=F32
        )
        total = term if total is None else total + term
    gated_grad_ref[...] = total
    for r, out_ref in enumerate(pieces):
        cols = at_block(me ^ r)
        out_ref[:, pl.ds(0, LANES)] = (gated_grad_ref[:, cols] * query_ref[:, cols].astype(F32)).astype(BF16)
        for k in range(width // LANES):
            out_ref[pl.ds(k * quarter, quarter), pl.ds(LANES, LANES)] = cot[
                me ^ r, at_block(part, quarter), pl.ds(k * LANES, LANES)
            ]


def quarter_kernel(seqs, *refs):
    held, out_ref = refs[:seqs], refs[-1]
    me = lax.axis_index("ctx")
    quarter = out_ref.shape[0] // seqs
    for r, ref in enumerate(held):
        for k in range(out_ref.shape[1] // LANES):
            out_ref[at_block(me ^ r, quarter), pl.ds(k * LANES, LANES)] = ref[
                pl.ds(k * quarter, quarter), pl.ds(LANES, LANES)
            ]


def output_kernel(seqs, *refs):
    held, (query_ref, gated_grad_ref, w_ref), refs = refs[:seqs], refs[seqs : seqs + 3], refs[seqs + 4 :]
    turned_ref, grad_query_ref, keep_ref, send_ref, whole = refs
    me, part = lax.axis_index("ctx"), lax.axis_index("tp")
    width = keep_ref.shape[2]
    for r, ref in enumerate(held):
        whole[:, at_block(me ^ r)] = ref[...]
    conv = whole[...].astype(F32)
    gated = query_ref[...].astype(F32) * conv
    turned_ref[...] = gated.T.astype(BF16)
    gated = gated.astype(BF16)
    grad_query_ref[...] = (gated_grad_ref[...] * conv).astype(BF16)
    for y in range(keep_ref.shape[0]):
        for ref, core in ((keep_ref, part & 1), (send_ref, (part & 1) ^ 1)):
            ref[y] = jnp.dot(gated, w_ref[:, at_block(2 * y + core, width)], preferred_element_type=F32)


def pair_kernel(keep_ref, other_ref, mine_ref, far_ref):
    y = lax.axis_index("tp") >> 1
    mine_ref[...] = keep_ref[y] + other_ref[y]
    far_ref[...] = (keep_ref[y ^ 1] + other_ref[y ^ 1]).astype(BF16)


def sum_kernel(mine_ref, other_ref, out_ref):
    out_ref[...] = (mine_ref[...] + other_ref[...].astype(F32)).astype(BF16)


def pass_kernel(one_ref, two_ref, *refs):
    one_out, two_out = refs[-2:]
    one_out[...] = one_ref[...]
    two_out[...] = two_ref[...]


def weight_kernel(own_ref, up_ref, down_ref, up2_ref, down2_ref, end_ref, cot_ref, *refs):
    out_ref, total, cot = refs[-3:]
    me = lax.axis_index("ctx")
    parts = cot_ref.shape[0]
    quarter = cot_ref.shape[1] // parts
    top = parts - 1

    def term(gated_ref, block):
        for p in range(parts):
            cot[pl.ds(p * quarter, quarter), :] = cot_ref[p, at_block(block, quarter), :]
        return jnp.dot(gated_ref[...], cot[...], preferred_element_type=F32)

    def add(gated_ref, block):
        total[...] += term(gated_ref, block)

    total[...] = term(own_ref, me)
    pl.when(me > 1)(lambda: add(up2_ref, me - 2))
    pl.when(me < top - 1)(lambda: add(down2_ref, me + 2))
    pl.when(me > 0)(lambda: add(up_ref, me - 1))
    pl.when(me < top)(lambda: add(down_ref, me + 1))
    pl.when(jnp.logical_or(me == 0, me == top))(lambda: add(end_ref, top - me))
    out_ref[...] = total[...].astype(BF16)


def add_kernel(factor, one_ref, other_ref, out_ref):
    out_ref[...] = (one_ref[...].astype(F32) + other_ref[...].astype(F32)) * factor


def mixed_kernel(seqs, *refs):
    held, (key_ref, value_ref, grad_key_ref, grad_value_ref, taps_ref) = refs[:seqs], refs[seqs:]
    me = lax.axis_index("ctx")
    for r, ref in enumerate(held):
        cols = at_block(me ^ r)
        mixed_grad = ref[:, pl.ds(0, LANES)].astype(F32)
        grad_key_ref[:, cols] = (mixed_grad * value_ref[:, cols].astype(F32)).astype(BF16)
        grad_value_ref[:, cols] = (mixed_grad * key_ref[:, cols].astype(F32)).astype(BF16)
        taps_ref[:, cols] = ref[:, pl.ds(LANES, LANES)]


def taps_kernel(factor, one_ref, other_ref, out_ref):
    out_ref[...] = (one_ref[...].astype(F32) + other_ref[...].astype(F32)).T * factor


def shape_of(shape, dtype):
    return jax.ShapeDtypeStruct(shape, dtype)


def call(kernel, outs, flops, moved, *args, scratch=(), left=(), room=20):
    vmem, anywhere = pl.BlockSpec(memory_space=pltpu.VMEM), pl.BlockSpec(memory_space=pl.ANY)
    return pl.pallas_call(
        kernel,
        out_shape=outs,
        in_specs=[anywhere if n in left else vmem for n in range(len(args))],
        out_specs=jax.tree.map(lambda _: vmem, outs),
        scratch_shapes=scratch,
        cost_estimate=pl.CostEstimate(flops=flops, bytes_accessed=moved, transcendentals=0),
        compiler_params=pltpu.CompilerParams(vmem_limit_bytes=room * 2**20),
    )(*args)


def exchange(pieces, axis):
    size = lax.axis_size(axis)
    return [pieces[0]] + [lax.ppermute(pieces[r], axis, [(d, d ^ r) for d in range(size)]) for r in range(1, size)]


def local_short(query_proj, key_proj, value_proj, filters, w_out, cotangent):
    query, key, value, cot = query_proj[0], key_proj[0], value_proj[0], cotangent[0]
    positions, channels = query.shape
    seqs, parts, pairs = lax.axis_size("ctx"), lax.axis_size("tp"), lax.axis_size("dp")
    blocks = positions * seqs // LANES
    features = w_out.shape[1]
    width = features // parts
    factor = 1.0 / math.sqrt(pairs * positions * seqs)
    tables = [jnp.asarray(m) for m in transform_tables(blocks)]
    ring = [(d, (d + 1) % pairs) for d in range(pairs)]
    table = (blocks + 1, 2 * LANES)
    one = [shape_of((positions, LANES), BF16)] * seqs
    two = [shape_of((positions, 2 * LANES), BF16)] * seqs
    rows = (positions, channels)
    line = seqs * positions

    cot_rows = exchange([cot] * parts, "tp")

    sent = call(
        prepare_kernel,
        two,
        10**6,
        2 * 10**6,
        key,
        value,
        filters,
        scratch=[
            pltpu.VMEM(rows, BF16),
            pltpu.VMEM(rows, BF16),
            pltpu.VMEM((channels, positions), F32),
            pltpu.SemaphoreType.DMA((3,)),
        ],
        left=(0, 1, 2),
        room=60,
    )
    held = exchange(sent, "ctx")

    gated_grad, *conv_grad = call(
        functools.partial(gradient_kernel, parts),
        [shape_of(rows, F32)] + two,
        2 * positions * channels * features,
        5 * 10**6,
        *cot_rows,
        w_out,
        query,
        *held[1:],
        scratch=[pltpu.VMEM((parts, positions, width), BF16)],
        left=range(parts + 2, parts + 5),
    )
    grad_held = exchange(conv_grad, "ctx")

    *conv_sent, spec = call(
        functools.partial(forward_kernel, seqs),
        one + [shape_of(table + (2 * LANES,), F32)],
        10**9,
        9 * 10**6,
        *held,
        *tables,
        conv_grad[1],
        scratch=[
            pltpu.VMEM((line, 2 * LANES), BF16),
            pltpu.VMEM(table + (2 * LANES,), BF16),
            pltpu.VMEM(table + (2 * LANES,), BF16),
            pltpu.VMEM(table + (LANES,), F32),
            pltpu.VMEM((line, LANES), BF16),
        ],
        left=(seqs + 2,),
    )
    conv = exchange(conv_sent, "ctx")


    cot_quarters = call(
        functools.partial(quarter_kernel, seqs),
        shape_of((positions, width), BF16),
        10**6,
        10**6,
        *grad_held,
        conv_sent[1],
        left=(seqs,),
    )
    cot_cols = lax.all_gather(cot_quarters, "tp")
    back_sent = call(
        functools.partial(backward_kernel, seqs),
        two,
        10**9,
        9 * 10**6,
        *grad_held,
        spec,
        *tables,
        conv_sent[1],
        cot_quarters,
        scratch=[
            pltpu.VMEM((line, LANES), BF16),
            pltpu.VMEM(table + (LANES,), BF16),
            pltpu.VMEM(table + (LANES,), BF16),
            pltpu.VMEM(table + (2 * LANES,), F32),
            pltpu.VMEM((line, 2 * LANES), BF16),
        ],
        left=(seqs + 3, seqs + 4),
    )
    back = exchange(back_sent, "ctx")

    turned, grad_query, share_kept, share_sent = call(
        functools.partial(output_kernel, seqs),
        [shape_of((channels, positions), BF16), shape_of(rows, BF16)] + [shape_of((parts // 2, positions, width), F32)] * 2,
        2 * positions * channels * features,
        5 * 10**6,
        *conv,
        query,
        gated_grad,
        w_out,
        back_sent[1],
        scratch=[pltpu.VMEM(rows, BF16)],
        left=(seqs + 3,),
    )
    up, down = [[(d, d + o) for d in range(seqs) if 0 <= d + o < seqs] for o in (1, -1)]
    above, below = lax.ppermute(turned, "ctx", up), lax.ppermute(turned, "ctx", down)
    across = lax.ppermute(turned, "ctx", [(0, seqs - 1), (seqs - 1, 0)])
    passed = call(pass_kernel, [shape_of((channels, positions), BF16)] * 2, 10**6, 10**6, above, below, back[1], left=(2,))
    above2, below2 = lax.ppermute(passed[0], "ctx", up[1:]), lax.ppermute(passed[1], "ctx", down[:-1])


    mine, far = call(
        pair_kernel,
        [shape_of((positions, width), F32), shape_of((positions, width), BF16)],
        10**6,
        3 * 10**6,
        share_kept,
        lax.ppermute(share_sent, "tp", [(j, j ^ 1) for j in range(parts)]),
    )
    far = lax.ppermute(far, "tp", [(j, j ^ 2) for j in range(parts)])
    output = call(sum_kernel, shape_of((positions, width), BF16), 10**6, 2 * 10**6, mine, far)

    grad_key, grad_value, taps = call(
        functools.partial(mixed_kernel, seqs),
        [shape_of(rows, BF16)] * 3,
        10**6,
        2 * 10**6,
        *back,
        key,
        value,
    )
    taps_other = lax.ppermute(taps, "dp", ring)
    weight_grad = call(
        weight_kernel,
        shape_of((channels, width), BF16),
        2 * line * channels * width,
        3 * 10**6,
        turned,
        above,
        below,
        above2,
        below2,
        across,
        cot_cols,
        taps_other,
        left=(7,),
        room=60,
        scratch=[pltpu.VMEM((channels, width), F32), pltpu.VMEM((positions, width), BF16)],
    )
    weight_other = lax.ppermute(weight_grad, "dp", ring)
    grad_wout = call(
        functools.partial(add_kernel, factor),
        shape_of((channels, width), F32),
        10**6,
        2 * 10**6,
        weight_grad,
        weight_other,
    )

    grad_filter = call(
        functools.partial(taps_kernel, factor),
        shape_of((channels, positions), F32),
        10**6,
        10**6,
        taps,
        taps_other,
    )
    return (output[None], grad_query[None], grad_key[None], grad_value[None], grad_filter, grad_wout)


def local(*args):
    positions, channels = args[0].shape[1:]
    seqs, parts, pairs = lax.axis_size("ctx"), lax.axis_size("tp"), lax.axis_size("dp")
    short = (
        channels == seqs * LANES
        and positions % LANES == 0
        and args[4].shape[1] == parts * parts * LANES
        and positions * seqs <= 8 * LANES
        and seqs == parts == 4
        and pairs == 2
    )
    return (local_short if short else local_any_length)(*args)


def solution(mesh):
    in_specs = (
        P("dp", "ctx", "tp"),
        P("dp", "ctx", "tp"),
        P("dp", "ctx", "tp"),
        P("tp", "ctx"),
        P("tp", None),
        P("dp", "ctx", "tp"),
    )
    out_specs = (
        P("dp", "ctx", "tp"),
        P("dp", "ctx", "tp"),
        P("dp", "ctx", "tp"),
        P("dp", "ctx", "tp"),
        P("tp", "ctx"),
        P("tp", "ctx"),
    )
    return jax.shard_map(local, mesh=mesh, in_specs=in_specs, out_specs=out_specs, check_vma=False)
```

```python
import functools
import math

import jax
import jax.numpy as jnp
import ml_dtypes
import numpy as np
from jax import lax
from jax.experimental import pallas as pl
from jax.experimental.pallas import tpu as pltpu
from jax.sharding import PartitionSpec as P

F32 = jnp.float32
BF16 = jnp.bfloat16
LANES = 128
ROWS = 16


def build_tables(length_fft):
    blocks = length_fft // 128
    outer = jnp.arange(blocks, dtype=jnp.int32)
    inner = jnp.arange(blocks // 2, dtype=jnp.int32)
    column = jnp.arange(128, dtype=jnp.int32)
    first = (outer[:, None] * inner[None, :] % blocks).astype(jnp.float32) * (
        -2.0 * math.pi / blocks
    )
    turned = (outer[:, None] * column[None, :] % length_fft).astype(jnp.float32) * (
        -2.0 * math.pi / length_fft
    )
    second = (column[:, None] * column[None, :] % 128).astype(jnp.float32) * (-2.0 * math.pi / 128)
    return (
        jnp.cos(first),
        jnp.sin(first),
        jnp.cos(turned),
        jnp.sin(turned),
        jnp.cos(second),
        jnp.sin(second),
    )


def product(form, left, right):
    return jnp.einsum(form, left, right, precision=lax.Precision.HIGHEST)


def forward_transform(signal, tables):
    cos_first, sin_first, cos_turn, sin_turn, cos_second, sin_second = tables
    real_one = product("ia,cab->cib", cos_first, signal)
    imag_one = product("ia,cab->cib", sin_first, signal)
    real_two = real_one * cos_turn - imag_one * sin_turn
    imag_two = real_one * sin_turn + imag_one * cos_turn
    real_out = product("cib,bj->cij", real_two, cos_second) - product(
        "cib,bj->cij", imag_two, sin_second
    )
    imag_out = product("cib,bj->cij", real_two, sin_second) + product(
        "cib,bj->cij", imag_two, cos_second
    )
    return (real_out, imag_out)


def inverse_transform(real_in, imag_in, tables, length_fft):
    cos_first, sin_first, cos_turn, sin_turn, cos_second, sin_second = tables
    real_one = product("cij,jb->cib", real_in, cos_second) + product(
        "cij,jb->cib", imag_in, sin_second
    )
    imag_one = product("cij,jb->cib", imag_in, cos_second) - product(
        "cij,jb->cib", real_in, sin_second
    )
    real_two = real_one * cos_turn + imag_one * sin_turn
    imag_two = imag_one * cos_turn - real_one * sin_turn
    result = product("ia,cib->cab", cos_first, real_two) + product(
        "ia,cib->cab", sin_first, imag_two
    )
    return result / length_fft


def local_any_length(query_proj, key_proj, value_proj, filters, w_out, cotangent):
    query_rows = query_proj[0].astype(jnp.float32)
    key_rows = key_proj[0].astype(jnp.float32)
    value_rows = value_proj[0].astype(jnp.float32)
    positions, channels = query_rows.shape
    seq_devices = lax.axis_size("ctx")
    length_fft = 2 * positions * seq_devices
    tables = build_tables(length_fft)
    mixed = (key_rows * value_rows).T
    mixed_chan, filter_chan = (
        lax.all_to_all(mixed, "ctx", split_axis=0, concat_axis=1, tiled=True),
        lax.all_to_all(filters, "ctx", split_axis=0, concat_axis=1, tiled=True),
    )
    local_channels = mixed_chan.shape[0]
    block_shape = (local_channels, length_fft // 256, 128)
    mixed_real, mixed_imag = forward_transform(mixed_chan.reshape(block_shape), tables)
    filter_real, filter_imag = forward_transform(filter_chan.reshape(block_shape), tables)
    conv_real = filter_real * mixed_real - filter_imag * mixed_imag
    conv_imag = filter_real * mixed_imag + filter_imag * mixed_real
    conv_chan = inverse_transform(conv_real, conv_imag, tables, length_fft).reshape(
        local_channels, -1
    )
    conv_back = lax.all_to_all(conv_chan, "ctx", split_axis=1, concat_axis=0, tiled=True)
    conv = conv_back.T
    gated = (query_rows * conv).astype(jnp.bfloat16)
    partial_terms = jnp.dot(gated, w_out, preferred_element_type=jnp.float32)
    output = lax.psum_scatter(partial_terms, "tp", scatter_dimension=1, tiled=True).astype(
        jnp.bfloat16
    )
    piece = lax.all_gather(cotangent[0], "tp", axis=1, tiled=True)
    grad_gated = lax.dot_general(
        piece, w_out, (((1,), (1,)), ((), ())), preferred_element_type=jnp.float32
    )
    weight_piece = lax.dot_general(
        gated, piece, (((0,), (0,)), ((), ())), preferred_element_type=jnp.float32
    )
    weight_grad = weight_piece
    grad_gated, weight_grad = (grad_gated, weight_grad)
    grad_query = (grad_gated * conv).astype(jnp.bfloat16)
    grad_conv = (grad_gated * query_rows).T
    grad_chan = lax.all_to_all(grad_conv, "ctx", split_axis=0, concat_axis=1, tiled=True)
    grad_real, grad_imag = forward_transform(grad_chan.reshape(block_shape), tables)
    back_real = filter_real * grad_real + filter_imag * grad_imag
    back_imag = filter_real * grad_imag - filter_imag * grad_real
    taps_real = grad_real * mixed_real + grad_imag * mixed_imag
    taps_imag = grad_imag * mixed_real - grad_real * mixed_imag
    mixed_grad_chan = inverse_transform(back_real, back_imag, tables, length_fft).reshape(
        local_channels, -1
    )
    filter_grad_chan = inverse_transform(taps_real, taps_imag, tables, length_fft).reshape(
        local_channels, -1
    )
    mixed_grad_back, filter_grad_back = (
        lax.all_to_all(mixed_grad_chan, "ctx", split_axis=1, concat_axis=0, tiled=True),
        lax.all_to_all(filter_grad_chan, "ctx", split_axis=1, concat_axis=0, tiled=True),
    )
    grad_mixed = mixed_grad_back.T
    grad_key = (grad_mixed * value_rows).astype(jnp.bfloat16)
    grad_value = (grad_mixed * key_rows).astype(jnp.bfloat16)
    factor = 1.0 / math.sqrt(lax.axis_size("dp") * positions * seq_devices)
    grad_filter = lax.psum(filter_grad_back, "dp") * factor
    summed_seq = lax.psum_scatter(weight_grad, "ctx", scatter_dimension=1, tiled=True)
    summed_weight = lax.psum(summed_seq, "dp")
    grad_wout = summed_weight * factor
    return (
        output[None],
        grad_query[None],
        grad_key[None],
        grad_value[None],
        grad_filter,
        grad_wout,
    )


@functools.lru_cache
def transform_tables(blocks):
    length_fft = 2 * blocks * LANES
    b = np.arange(LANES, dtype=np.int64)
    angle = (2.0 * math.pi / LANES) * (b[:, None] * b[None, :] % LANES)
    cos, sin = np.cos(angle), np.sin(angle)
    whole = np.block([[cos, sin], [-sin, cos]])
    high = whole.astype(ml_dtypes.bfloat16)
    low = (whole - high.astype(np.float64)).astype(ml_dtypes.bfloat16)
    turn = np.zeros((LANES, LANES))
    i = np.arange(blocks + 1)
    angle = (2.0 * math.pi / length_fft) * (b[:, None] * i[None, :] % length_fft)
    turn[:, : blocks + 1] = np.cos(angle)
    turn[:, LANES // 2 : LANES // 2 + blocks + 1] = np.sin(angle)
    return np.stack([high, low]), turn.astype(np.float32)


def scaled_sum(terms):
    total = None
    for factor, term in terms:
        if abs(factor) < 1e-9:
            continue
        if abs(factor - 1.0) < 1e-9:
            total = term if total is None else total + term
        elif abs(factor + 1.0) < 1e-9:
            total = -term if total is None else total - term
        else:
            total = factor * term if total is None else total + factor * term
    return total


def split_bf16(value):
    high = value.astype(BF16)
    return high, (value - high.astype(F32)).astype(BF16)


def product3(matrix_ref, high, low):
    dot = functools.partial(jnp.dot, preferred_element_type=F32)
    return dot(matrix_ref[0], high) + (dot(matrix_ref[0], low) + dot(matrix_ref[1], high))


def turn_of(turn_ref, i, row):
    rows = pl.ds(row, ROWS)
    cos = turn_ref[rows, i : i + 1]
    sin = turn_ref[rows, LANES // 2 + i : LANES // 2 + i + 1]
    return jnp.broadcast_to(cos, (ROWS, LANES)), jnp.broadcast_to(sin, (ROWS, LANES))


def each_chunk(lanes, body):
    @pl.loop(0, LANES // ROWS, unroll=2)
    def _(step):
        for lane in range(0, lanes, LANES):
            body(pl.multiple_of(step * ROWS, ROWS), lane)


def over_blocks(read, blocks, lanes, turn_ref, high, low):
    def chunk(row, lane):
        def put(i, real, imag):
            if i > 0:
                cos, sin = turn_of(turn_ref, i, row)
                if imag is None:
                    real, imag = real * cos, -(real * sin)
                else:
                    real, imag = real * cos + imag * sin, imag * cos - real * sin
            for part, value in ((0, real), (1, jnp.zeros_like(real) if imag is None else imag)):
                top, rest = split_bf16(value)
                rows = pl.ds(pl.multiple_of(part * LANES + row, ROWS), ROWS)
                high[i, rows, pl.ds(lane, LANES)] = top
                low[i, rows, pl.ds(lane, LANES)] = rest

        slabs = [read(a, row, lane) for a in range(blocks)]
        for i in range(blocks // 2 + 1):
            sums = []
            for first in (0, 1):
                picked = range(first, blocks, 2)
                angle = [math.pi * ((i * a) % (2 * blocks)) / blocks for a in picked]
                sums.append(scaled_sum([(math.cos(g), slabs[a]) for g, a in zip(angle, picked)]))
                sums.append(scaled_sum([(-math.sin(g), slabs[a]) for g, a in zip(angle, picked)]))
            even_real, even_imag, odd_real, odd_imag = sums

            def joined(one, other, sign):
                if one is None or other is None:
                    return one if other is None else (other if sign > 0 else -other)
                return one + other if sign > 0 else one - other

            put(i, joined(even_real, odd_real, 1), joined(even_imag, odd_imag, 1))
            if blocks - i != i:
                put(blocks - i, joined(even_real, odd_real, -1), joined(odd_imag, even_imag, -1))

    each_chunk(lanes, chunk)


def back_to_blocks(turned, blocks, lanes, turn_ref, write):
    scale = 1.0 / (blocks * LANES)

    def chunk(row, lane):
        def get(i):
            real = turned[i, pl.ds(row, ROWS), pl.ds(lane, LANES)]
            imag = -turned[i, pl.ds(pl.multiple_of(LANES + row, ROWS), ROWS), pl.ds(lane, LANES)]
            if i > 0:
                cos, sin = turn_of(turn_ref, i, row)
                real, imag = real * cos - imag * sin, imag * cos + real * sin
            return real, imag

        terms = [[] for _ in range(blocks)]
        for i in range(blocks // 2 + 1):
            real, imag = get(i)
            if blocks - i != i:
                other_real, other_imag = get(blocks - i)
                pairs = ((real + other_real, imag - other_imag), (real - other_real, imag + other_imag))
            else:
                pairs = ((real, imag), (real, imag))
            if i == 0:
                pairs = tuple((0.5 * one, 0.5 * two) for one, two in pairs)
            for a in range(blocks):
                angle = math.pi * ((i * a) % (2 * blocks)) / blocks
                terms[a].append((math.cos(angle), pairs[a % 2][0]))
                terms[a].append((-math.sin(angle), pairs[a % 2][1]))
        for a in range(blocks):
            write(a, row, lane, scaled_sum(terms[a]) * scale)

    each_chunk(lanes, chunk)


def at_block(index, size=LANES):
    return pl.ds(pl.multiple_of(index * size, size), size)


def reader(ref):
    def read(a, row, lane):
        rows = pl.ds(pl.multiple_of(a * LANES + row, ROWS), ROWS)
        return ref[rows, pl.ds(lane, LANES)].astype(F32)

    return read


def writer(ref):
    def write(a, row, lane, value):
        rows = pl.ds(pl.multiple_of(a * LANES + row, ROWS), ROWS)
        ref[rows, pl.ds(lane, LANES)] = value.astype(ref.dtype)

    return write


def place_pieces(pieces, whole):
    me = lax.axis_index("ctx")
    for r, ref in enumerate(pieces):
        whole[at_block(me ^ r, ref.shape[0]), :] = ref[:, pl.ds(0, whole.shape[1])]


def take_pieces(whole, pieces):
    me = lax.axis_index("ctx")
    for r, ref in enumerate(pieces):
        ref[...] = whole[at_block(me ^ r, ref.shape[0]), :]


def fetch(pairs, sems):
    copies = [pltpu.make_async_copy(source, target, sems.at[n]) for n, (source, target) in enumerate(pairs)]
    for copy in copies:
        copy.start()
    return copies


def prepare_kernel(*refs):
    *pieces, key_ref, value_ref, filter_ref, sems = refs[3:]
    for copy in fetch(list(zip(refs[:3], (key_ref, value_ref, filter_ref))), sems):
        copy.wait()
    me = lax.axis_index("ctx")
    for r, out_ref in enumerate(pieces):
        cols = at_block(me ^ r)
        mixed = key_ref[:, cols].astype(F32) * value_ref[:, cols].astype(F32)
        out_ref[:, pl.ds(0, LANES)] = mixed.astype(BF16)
        out_ref[:, pl.ds(LANES, LANES)] = filter_ref[cols, :].T.astype(BF16)


def forward_kernel(seqs, *refs):
    held, (matrix, turn), refs = refs[:seqs], refs[seqs : seqs + 2], refs[seqs + 3 :]
    sent, (spec_ref, whole, zh, zl, turned, conv) = refs[:seqs], refs[seqs:]
    blocks = spec_ref.shape[0] - 1
    place_pieces(held, whole)
    over_blocks(reader(whole), blocks, 2 * LANES, turn, zh, zl)
    for i in range(blocks + 1):
        spec = product3(matrix, zh[i], zl[i])
        spec_ref[i] = spec
        mixed_real, mixed_imag = spec[:LANES, :LANES], spec[LANES:, :LANES]
        filter_real, filter_imag = spec[:LANES, LANES:], spec[LANES:, LANES:]
        real = filter_real * mixed_real - filter_imag * mixed_imag
        imag = filter_real * mixed_imag + filter_imag * mixed_real
        turned[i] = product3(matrix, *split_bf16(jnp.concatenate([real, -imag], axis=0)))
    back_to_blocks(turned, blocks, LANES, turn, writer(conv))
    take_pieces(conv, sent)


def backward_kernel(seqs, *refs):
    held, (spec_ref, matrix, turn), refs = refs[:seqs], refs[seqs : seqs + 3], refs[seqs + 5 :]
    sent, (whole, zh, zl, turned, back) = refs[:seqs], refs[seqs:]
    blocks = spec_ref.shape[0] - 1
    place_pieces(held, whole)
    over_blocks(reader(whole), blocks, LANES, turn, zh, zl)
    for i in range(blocks + 1):
        grad = product3(matrix, zh[i], zl[i])
        grad_real, grad_imag = grad[:LANES], grad[LANES:]
        mixed_real, mixed_imag = spec_ref[i, :LANES, :LANES], spec_ref[i, LANES:, :LANES]
        filter_real, filter_imag = spec_ref[i, :LANES, LANES:], spec_ref[i, LANES:, LANES:]
        back_real = filter_real * grad_real + filter_imag * grad_imag
        back_imag = filter_imag * grad_real - filter_real * grad_imag
        taps_real = grad_real * mixed_real + grad_imag * mixed_imag
        taps_imag = grad_real * mixed_imag - grad_imag * mixed_real
        real = jnp.concatenate([back_real, taps_real], axis=1)
        imag = jnp.concatenate([back_imag, taps_imag], axis=1)
        turned[i] = product3(matrix, *split_bf16(jnp.concatenate([real, imag], axis=0)))
    back_to_blocks(turned, blocks, 2 * LANES, turn, writer(back))
    take_pieces(back, sent)


def gradient_kernel(parts, *refs):
    cots, (w_ref, query_ref), refs = refs[:parts], refs[parts : parts + 2], refs[parts + 3 :]
    gated_grad_ref, *pieces, cot = refs
    me, part = lax.axis_index("ctx"), lax.axis_index("tp")
    positions, width = cots[0].shape
    quarter = positions // parts
    total = None
    for r, ref in enumerate(cots):
        cot[part ^ r] = ref[...]
        term = lax.dot_general(
            ref[...], w_ref[:, at_block(part ^ r, width)], (((1,), (1,)), ((), ())), preferred_element_type=F32
        )
        total = term if total is None else total + term
    gated_grad_ref[...] = total
    for r, out_ref in enumerate(pieces):
        cols = at_block(me ^ r)
        out_ref[:, pl.ds(0, LANES)] = (gated_grad_ref[:, cols] * query_ref[:, cols].astype(F32)).astype(BF16)
        for k in range(width // LANES):
            out_ref[pl.ds(k * quarter, quarter), pl.ds(LANES, LANES)] = cot[
                me ^ r, at_block(part, quarter), pl.ds(k * LANES, LANES)
            ]


def quarter_kernel(seqs, *refs):
    held, out_ref = refs[:seqs], refs[-1]
    me = lax.axis_index("ctx")
    quarter = out_ref.shape[0] // seqs
    for r, ref in enumerate(held):
        for k in range(out_ref.shape[1] // LANES):
            out_ref[at_block(me ^ r, quarter), pl.ds(k * LANES, LANES)] = ref[
                pl.ds(k * quarter, quarter), pl.ds(LANES, LANES)
            ]


def output_kernel(seqs, *refs):
    held, (query_ref, gated_grad_ref, w_ref), refs = refs[:seqs], refs[seqs : seqs + 3], refs[seqs + 4 :]
    turned_ref, grad_query_ref, keep_ref, send_ref, whole = refs
    me, part = lax.axis_index("ctx"), lax.axis_index("tp")
    width = keep_ref.shape[2]
    for r, ref in enumerate(held):
        whole[:, at_block(me ^ r)] = ref[...]
    conv = whole[...].astype(F32)
    gated = query_ref[...].astype(F32) * conv
    turned_ref[...] = gated.T.astype(BF16)
    gated = gated.astype(BF16)
    grad_query_ref[...] = (gated_grad_ref[...] * conv).astype(BF16)
    for y in range(keep_ref.shape[0]):
        for ref, core in ((keep_ref, part & 1), (send_ref, (part & 1) ^ 1)):
            ref[y] = jnp.dot(gated, w_ref[:, at_block(2 * y + core, width)], preferred_element_type=F32)


def pair_kernel(keep_ref, other_ref, mine_ref, far_ref):
    y = lax.axis_index("tp") >> 1
    mine_ref[...] = keep_ref[y] + other_ref[y]
    far_ref[...] = (keep_ref[y ^ 1] + other_ref[y ^ 1]).astype(BF16)


def sum_kernel(mine_ref, other_ref, out_ref):
    out_ref[...] = (mine_ref[...] + other_ref[...].astype(F32)).astype(BF16)


def pass_kernel(one_ref, _, out_ref):
    out_ref[...] = one_ref[...]


def weight_kernel(seqs, *refs):
    pieces, cot_ref, (out_ref, cot) = refs[:seqs], refs[seqs], refs[-2:]
    me = lax.axis_index("ctx")
    parts = cot_ref.shape[0]
    quarter = cot_ref.shape[1] // parts
    total = None
    for r, ref in enumerate(pieces):
        for p in range(parts):
            cot[r, pl.ds(p * quarter, quarter), :] = cot_ref[p, at_block(me ^ r, quarter), :]
        term = jnp.dot(ref[...], cot[r], preferred_element_type=F32)
        total = term if total is None else total + term
    out_ref[...] = total.astype(BF16)


def add_kernel(factor, one_ref, other_ref, out_ref):
    out_ref[...] = (one_ref[...].astype(F32) + other_ref[...].astype(F32)) * factor


def mixed_kernel(seqs, *refs):
    held, (key_ref, value_ref, grad_key_ref, grad_value_ref, taps_ref) = refs[:seqs], refs[seqs:]
    me = lax.axis_index("ctx")
    for r, ref in enumerate(held):
        cols = at_block(me ^ r)
        mixed_grad = ref[:, pl.ds(0, LANES)].astype(F32)
        grad_key_ref[:, cols] = (mixed_grad * value_ref[:, cols].astype(F32)).astype(BF16)
        grad_value_ref[:, cols] = (mixed_grad * key_ref[:, cols].astype(F32)).astype(BF16)
        taps_ref[:, cols] = ref[:, pl.ds(LANES, LANES)]


def taps_kernel(factor, one_ref, other_ref, out_ref):
    out_ref[...] = (one_ref[...].astype(F32) + other_ref[...].astype(F32)).T * factor


def shape_of(shape, dtype):
    return jax.ShapeDtypeStruct(shape, dtype)


def call(kernel, outs, flops, moved, *args, scratch=(), left=(), room=20):
    vmem, anywhere = pl.BlockSpec(memory_space=pltpu.VMEM), pl.BlockSpec(memory_space=pl.ANY)
    return pl.pallas_call(
        kernel,
        out_shape=outs,
        in_specs=[anywhere if n in left else vmem for n in range(len(args))],
        out_specs=jax.tree.map(lambda _: vmem, outs),
        scratch_shapes=scratch,
        cost_estimate=pl.CostEstimate(flops=flops, bytes_accessed=moved, transcendentals=0),
        compiler_params=pltpu.CompilerParams(vmem_limit_bytes=room * 2**20),
    )(*args)


def exchange(pieces, axis):
    size = lax.axis_size(axis)
    return [pieces[0]] + [lax.ppermute(pieces[r], axis, [(d, d ^ r) for d in range(size)]) for r in range(1, size)]


def local_short(query_proj, key_proj, value_proj, filters, w_out, cotangent):
    query, key, value, cot = query_proj[0], key_proj[0], value_proj[0], cotangent[0]
    positions, channels = query.shape
    seqs, parts, pairs = lax.axis_size("ctx"), lax.axis_size("tp"), lax.axis_size("dp")
    blocks = positions * seqs // LANES
    features = w_out.shape[1]
    width = features // parts
    factor = 1.0 / math.sqrt(pairs * positions * seqs)
    tables = [jnp.asarray(m) for m in transform_tables(blocks)]
    ring = [(d, (d + 1) % pairs) for d in range(pairs)]
    table = (blocks + 1, 2 * LANES)
    one = [shape_of((positions, LANES), BF16)] * seqs
    two = [shape_of((positions, 2 * LANES), BF16)] * seqs
    rows = (positions, channels)
    line = seqs * positions

    cot_rows = exchange([cot] * parts, "tp")

    sent = call(
        prepare_kernel,
        two,
        10**6,
        2 * 10**6,
        key,
        value,
        filters,
        scratch=[
            pltpu.VMEM(rows, BF16),
            pltpu.VMEM(rows, BF16),
            pltpu.VMEM((channels, positions), F32),
            pltpu.SemaphoreType.DMA((3,)),
        ],
        left=(0, 1, 2),
        room=60,
    )
    held = exchange(sent, "ctx")

    gated_grad, *conv_grad = call(
        functools.partial(gradient_kernel, parts),
        [shape_of(rows, F32)] + two,
        2 * positions * channels * features,
        5 * 10**6,
        *cot_rows,
        w_out,
        query,
        held[1],
        scratch=[pltpu.VMEM((parts, positions, width), BF16)],
        left=(parts + 2,),
    )
    grad_held = exchange(conv_grad, "ctx")

    *conv_sent, spec = call(
        functools.partial(forward_kernel, seqs),
        one + [shape_of(table + (2 * LANES,), F32)],
        10**9,
        9 * 10**6,
        *held,
        *tables,
        conv_grad[1],
        scratch=[
            pltpu.VMEM((line, 2 * LANES), BF16),
            pltpu.VMEM(table + (2 * LANES,), BF16),
            pltpu.VMEM(table + (2 * LANES,), BF16),
            pltpu.VMEM(table + (LANES,), F32),
            pltpu.VMEM((line, LANES), BF16),
        ],
        left=(seqs + 2,),
    )
    conv = exchange(conv_sent, "ctx")


    cot_quarters = call(
        functools.partial(quarter_kernel, seqs),
        shape_of((positions, width), BF16),
        10**6,
        10**6,
        *grad_held,
        conv_sent[1],
        left=(seqs,),
    )
    cot_cols = lax.all_gather(cot_quarters, "tp")
    back_sent = call(
        functools.partial(backward_kernel, seqs),
        two,
        10**9,
        9 * 10**6,
        *grad_held,
        spec,
        *tables,
        conv_sent[1],
        cot_quarters,
        scratch=[
            pltpu.VMEM((line, LANES), BF16),
            pltpu.VMEM(table + (LANES,), BF16),
            pltpu.VMEM(table + (LANES,), BF16),
            pltpu.VMEM(table + (2 * LANES,), F32),
            pltpu.VMEM((line, 2 * LANES), BF16),
        ],
        left=(seqs + 3, seqs + 4),
    )
    back = exchange(back_sent, "ctx")

    turned, grad_query, share_kept, share_sent = call(
        functools.partial(output_kernel, seqs),
        [shape_of((channels, positions), BF16), shape_of(rows, BF16)] + [shape_of((parts // 2, positions, width), F32)] * 2,
        2 * positions * channels * features,
        5 * 10**6,
        *conv,
        query,
        gated_grad,
        w_out,
        back_sent[1],
        scratch=[pltpu.VMEM(rows, BF16)],
        left=(seqs + 3,),
    )
    first, third = [[(d, d ^ r) for d in range(seqs)] for r in (1, 3)]
    across = lax.ppermute(turned, "ctx", third)
    near = lax.ppermute(turned, "ctx", first)
    passed = call(pass_kernel, shape_of((channels, positions), BF16), 10**6, 10**6, across, back[1], left=(1,))
    gathered = [turned, near, lax.ppermute(passed, "ctx", first), across]
    mine, far = call(
        pair_kernel,
        [shape_of((positions, width), F32), shape_of((positions, width), BF16)],
        10**6,
        3 * 10**6,
        share_kept,
        lax.ppermute(share_sent, "tp", [(j, j ^ 1) for j in range(parts)]),
    )
    far = lax.ppermute(far, "tp", [(j, j ^ 2) for j in range(parts)])
    output = call(sum_kernel, shape_of((positions, width), BF16), 10**6, 2 * 10**6, mine, far)

    grad_key, grad_value, taps = call(
        functools.partial(mixed_kernel, seqs),
        [shape_of(rows, BF16)] * 3,
        10**6,
        2 * 10**6,
        *back,
        key,
        value,
    )
    taps_other = lax.ppermute(taps, "dp", ring)
    weight_grad = call(
        functools.partial(weight_kernel, seqs),
        shape_of((channels, width), BF16),
        2 * line * channels * width,
        3 * 10**6,
        *gathered,
        cot_cols,
        back[2],
        left=(seqs + 1,),
        room=60,
        scratch=[pltpu.VMEM((seqs, positions, width), BF16)],
    )
    weight_other = lax.ppermute(weight_grad, "dp", ring)
    grad_wout = call(
        functools.partial(add_kernel, factor),
        shape_of((channels, width), F32),
        10**6,
        2 * 10**6,
        weight_grad,
        weight_other,
    )

    grad_filter = call(
        functools.partial(taps_kernel, factor),
        shape_of((channels, positions), F32),
        10**6,
        10**6,
        taps,
        taps_other,
    )
    return (output[None], grad_query[None], grad_key[None], grad_value[None], grad_filter, grad_wout)


def local(*args):
    positions, channels = args[0].shape[1:]
    seqs, parts, pairs = lax.axis_size("ctx"), lax.axis_size("tp"), lax.axis_size("dp")
    short = (
        channels == seqs * LANES
        and positions % LANES == 0
        and args[4].shape[1] == parts * parts * LANES
        and positions * seqs <= 8 * LANES
        and seqs == parts == 4
        and pairs == 2
    )
    return (local_short if short else local_any_length)(*args)


def solution(mesh):
    in_specs = (
        P("dp", "ctx", "tp"),
        P("dp", "ctx", "tp"),
        P("dp", "ctx", "tp"),
        P("tp", "ctx"),
        P("tp", None),
        P("dp", "ctx", "tp"),
    )
    out_specs = (
        P("dp", "ctx", "tp"),
        P("dp", "ctx", "tp"),
        P("dp", "ctx", "tp"),
        P("dp", "ctx", "tp"),
        P("tp", "ctx"),
        P("tp", "ctx"),
    )
    return jax.shard_map(local, mesh=mesh, in_specs=in_specs, out_specs=out_specs, check_vma=False)
```

```python
import functools
import math

import jax
import jax.numpy as jnp
import ml_dtypes
import numpy as np
from jax import lax
from jax.experimental import pallas as pl
from jax.experimental.pallas import tpu as pltpu
from jax.sharding import PartitionSpec as P

F32 = jnp.float32
BF16 = jnp.bfloat16
LANES = 128
ROWS = 16


def build_tables(length_fft):
    blocks = length_fft // 128
    outer = jnp.arange(blocks, dtype=jnp.int32)
    inner = jnp.arange(blocks // 2, dtype=jnp.int32)
    column = jnp.arange(128, dtype=jnp.int32)
    first = (outer[:, None] * inner[None, :] % blocks).astype(jnp.float32) * (
        -2.0 * math.pi / blocks
    )
    turned = (outer[:, None] * column[None, :] % length_fft).astype(jnp.float32) * (
        -2.0 * math.pi / length_fft
    )
    second = (column[:, None] * column[None, :] % 128).astype(jnp.float32) * (-2.0 * math.pi / 128)
    return (
        jnp.cos(first),
        jnp.sin(first),
        jnp.cos(turned),
        jnp.sin(turned),
        jnp.cos(second),
        jnp.sin(second),
    )


def product(form, left, right):
    return jnp.einsum(form, left, right, precision=lax.Precision.HIGHEST)


def forward_transform(signal, tables):
    cos_first, sin_first, cos_turn, sin_turn, cos_second, sin_second = tables
    real_one = product("ia,cab->cib", cos_first, signal)
    imag_one = product("ia,cab->cib", sin_first, signal)
    real_two = real_one * cos_turn - imag_one * sin_turn
    imag_two = real_one * sin_turn + imag_one * cos_turn
    real_out = product("cib,bj->cij", real_two, cos_second) - product(
        "cib,bj->cij", imag_two, sin_second
    )
    imag_out = product("cib,bj->cij", real_two, sin_second) + product(
        "cib,bj->cij", imag_two, cos_second
    )
    return (real_out, imag_out)


def inverse_transform(real_in, imag_in, tables, length_fft):
    cos_first, sin_first, cos_turn, sin_turn, cos_second, sin_second = tables
    real_one = product("cij,jb->cib", real_in, cos_second) + product(
        "cij,jb->cib", imag_in, sin_second
    )
    imag_one = product("cij,jb->cib", imag_in, cos_second) - product(
        "cij,jb->cib", real_in, sin_second
    )
    real_two = real_one * cos_turn + imag_one * sin_turn
    imag_two = imag_one * cos_turn - real_one * sin_turn
    result = product("ia,cib->cab", cos_first, real_two) + product(
        "ia,cib->cab", sin_first, imag_two
    )
    return result / length_fft


def local_any_length(query_proj, key_proj, value_proj, filters, w_out, cotangent):
    query_rows = query_proj[0].astype(jnp.float32)
    key_rows = key_proj[0].astype(jnp.float32)
    value_rows = value_proj[0].astype(jnp.float32)
    positions, channels = query_rows.shape
    seq_devices = lax.axis_size("ctx")
    length_fft = 2 * positions * seq_devices
    tables = build_tables(length_fft)
    mixed = (key_rows * value_rows).T
    mixed_chan, filter_chan = (
        lax.all_to_all(mixed, "ctx", split_axis=0, concat_axis=1, tiled=True),
        lax.all_to_all(filters, "ctx", split_axis=0, concat_axis=1, tiled=True),
    )
    local_channels = mixed_chan.shape[0]
    block_shape = (local_channels, length_fft // 256, 128)
    mixed_real, mixed_imag = forward_transform(mixed_chan.reshape(block_shape), tables)
    filter_real, filter_imag = forward_transform(filter_chan.reshape(block_shape), tables)
    conv_real = filter_real * mixed_real - filter_imag * mixed_imag
    conv_imag = filter_real * mixed_imag + filter_imag * mixed_real
    conv_chan = inverse_transform(conv_real, conv_imag, tables, length_fft).reshape(
        local_channels, -1
    )
    conv_back = lax.all_to_all(conv_chan, "ctx", split_axis=1, concat_axis=0, tiled=True)
    conv = conv_back.T
    gated = (query_rows * conv).astype(jnp.bfloat16)
    partial_terms = jnp.dot(gated, w_out, preferred_element_type=jnp.float32)
    output = lax.psum_scatter(partial_terms, "tp", scatter_dimension=1, tiled=True).astype(
        jnp.bfloat16
    )
    piece = lax.all_gather(cotangent[0], "tp", axis=1, tiled=True)
    grad_gated = lax.dot_general(
        piece, w_out, (((1,), (1,)), ((), ())), preferred_element_type=jnp.float32
    )
    weight_piece = lax.dot_general(
        gated, piece, (((0,), (0,)), ((), ())), preferred_element_type=jnp.float32
    )
    weight_grad = weight_piece
    grad_gated, weight_grad = (grad_gated, weight_grad)
    grad_query = (grad_gated * conv).astype(jnp.bfloat16)
    grad_conv = (grad_gated * query_rows).T
    grad_chan = lax.all_to_all(grad_conv, "ctx", split_axis=0, concat_axis=1, tiled=True)
    grad_real, grad_imag = forward_transform(grad_chan.reshape(block_shape), tables)
    back_real = filter_real * grad_real + filter_imag * grad_imag
    back_imag = filter_real * grad_imag - filter_imag * grad_real
    taps_real = grad_real * mixed_real + grad_imag * mixed_imag
    taps_imag = grad_imag * mixed_real - grad_real * mixed_imag
    mixed_grad_chan = inverse_transform(back_real, back_imag, tables, length_fft).reshape(
        local_channels, -1
    )
    filter_grad_chan = inverse_transform(taps_real, taps_imag, tables, length_fft).reshape(
        local_channels, -1
    )
    mixed_grad_back, filter_grad_back = (
        lax.all_to_all(mixed_grad_chan, "ctx", split_axis=1, concat_axis=0, tiled=True),
        lax.all_to_all(filter_grad_chan, "ctx", split_axis=1, concat_axis=0, tiled=True),
    )
    grad_mixed = mixed_grad_back.T
    grad_key = (grad_mixed * value_rows).astype(jnp.bfloat16)
    grad_value = (grad_mixed * key_rows).astype(jnp.bfloat16)
    factor = 1.0 / math.sqrt(lax.axis_size("dp") * positions * seq_devices)
    grad_filter = lax.psum(filter_grad_back, "dp") * factor
    summed_seq = lax.psum_scatter(weight_grad, "ctx", scatter_dimension=1, tiled=True)
    summed_weight = lax.psum(summed_seq, "dp")
    grad_wout = summed_weight * factor
    return (
        output[None],
        grad_query[None],
        grad_key[None],
        grad_value[None],
        grad_filter,
        grad_wout,
    )


@functools.lru_cache
def transform_tables(blocks):
    length_fft = 2 * blocks * LANES
    b = np.arange(LANES, dtype=np.int64)
    angle = (2.0 * math.pi / LANES) * (b[:, None] * b[None, :] % LANES)
    cos, sin = np.cos(angle), np.sin(angle)
    whole = np.block([[cos, sin], [-sin, cos]])
    high = whole.astype(ml_dtypes.bfloat16)
    low = (whole - high.astype(np.float64)).astype(ml_dtypes.bfloat16)
    turn = np.zeros((LANES, LANES))
    i = np.arange(blocks + 1)
    angle = (2.0 * math.pi / length_fft) * (b[:, None] * i[None, :] % length_fft)
    turn[:, : blocks + 1] = np.cos(angle)
    turn[:, LANES // 2 : LANES // 2 + blocks + 1] = np.sin(angle)
    return np.stack([high, low]), turn.astype(np.float32)


def scaled_sum(terms):
    total = None
    for factor, term in terms:
        if abs(factor) < 1e-9:
            continue
        if abs(factor - 1.0) < 1e-9:
            total = term if total is None else total + term
        elif abs(factor + 1.0) < 1e-9:
            total = -term if total is None else total - term
        else:
            total = factor * term if total is None else total + factor * term
    return total


def split_bf16(value):
    high = value.astype(BF16)
    return high, (value - high.astype(F32)).astype(BF16)


def product3(matrix_ref, high, low):
    dot = functools.partial(jnp.dot, preferred_element_type=F32)
    return dot(matrix_ref[0], high) + (dot(matrix_ref[0], low) + dot(matrix_ref[1], high))


def turn_of(turn_ref, i, row):
    rows = pl.ds(row, ROWS)
    cos = turn_ref[rows, i : i + 1]
    sin = turn_ref[rows, LANES // 2 + i : LANES // 2 + i + 1]
    return jnp.broadcast_to(cos, (ROWS, LANES)), jnp.broadcast_to(sin, (ROWS, LANES))


def each_chunk(lanes, body):
    @pl.loop(0, LANES // ROWS, unroll=4)
    def _(step):
        for lane in range(0, lanes, LANES):
            body(pl.multiple_of(step * ROWS, ROWS), lane)


def over_blocks(read, blocks, lanes, turn_ref, high, low):
    def chunk(row, lane):
        def put(i, real, imag):
            if i > 0:
                cos, sin = turn_of(turn_ref, i, row)
                if imag is None:
                    real, imag = real * cos, -(real * sin)
                else:
                    real, imag = real * cos + imag * sin, imag * cos - real * sin
            for part, value in ((0, real), (1, jnp.zeros_like(real) if imag is None else imag)):
                top, rest = split_bf16(value)
                rows = pl.ds(pl.multiple_of(part * LANES + row, ROWS), ROWS)
                high[i, rows, pl.ds(lane, LANES)] = top
                low[i, rows, pl.ds(lane, LANES)] = rest

        slabs = [read(a, row, lane) for a in range(blocks)]
        for i in range(blocks // 2 + 1):
            sums = []
            for first in (0, 1):
                picked = range(first, blocks, 2)
                angle = [math.pi * ((i * a) % (2 * blocks)) / blocks for a in picked]
                sums.append(scaled_sum([(math.cos(g), slabs[a]) for g, a in zip(angle, picked)]))
                sums.append(scaled_sum([(-math.sin(g), slabs[a]) for g, a in zip(angle, picked)]))
            even_real, even_imag, odd_real, odd_imag = sums

            def joined(one, other, sign):
                if one is None or other is None:
                    return one if other is None else (other if sign > 0 else -other)
                return one + other if sign > 0 else one - other

            put(i, joined(even_real, odd_real, 1), joined(even_imag, odd_imag, 1))
            if blocks - i != i:
                put(blocks - i, joined(even_real, odd_real, -1), joined(odd_imag, even_imag, -1))

    each_chunk(lanes, chunk)


def back_to_blocks(turned, blocks, lanes, turn_ref, write):
    scale = 1.0 / (blocks * LANES)

    def chunk(row, lane):
        def get(i):
            real = turned[i, pl.ds(row, ROWS), pl.ds(lane, LANES)]
            imag = -turned[i, pl.ds(pl.multiple_of(LANES + row, ROWS), ROWS), pl.ds(lane, LANES)]
            if i > 0:
                cos, sin = turn_of(turn_ref, i, row)
                real, imag = real * cos - imag * sin, imag * cos + real * sin
            return real, imag

        terms = [[] for _ in range(blocks)]
        for i in range(blocks // 2 + 1):
            real, imag = get(i)
            if blocks - i != i:
                other_real, other_imag = get(blocks - i)
                pairs = ((real + other_real, imag - other_imag), (real - other_real, imag + other_imag))
            else:
                pairs = ((real, imag), (real, imag))
            if i == 0:
                pairs = tuple((0.5 * one, 0.5 * two) for one, two in pairs)
            for a in range(blocks):
                angle = math.pi * ((i * a) % (2 * blocks)) / blocks
                terms[a].append((math.cos(angle), pairs[a % 2][0]))
                terms[a].append((-math.sin(angle), pairs[a % 2][1]))
        for a in range(blocks):
            write(a, row, lane, scaled_sum(terms[a]) * scale)

    each_chunk(lanes, chunk)


def at_block(index, size=LANES):
    return pl.ds(pl.multiple_of(index * size, size), size)


def reader(ref):
    def read(a, row, lane):
        rows = pl.ds(pl.multiple_of(a * LANES + row, ROWS), ROWS)
        return ref[rows, pl.ds(lane, LANES)].astype(F32)

    return read


def writer(ref):
    def write(a, row, lane, value):
        rows = pl.ds(pl.multiple_of(a * LANES + row, ROWS), ROWS)
        ref[rows, pl.ds(lane, LANES)] = value.astype(ref.dtype)

    return write


def place_pieces(pieces, whole):
    me = lax.axis_index("ctx")
    for r, ref in enumerate(pieces):
        whole[at_block(me ^ r, ref.shape[0]), :] = ref[:, pl.ds(0, whole.shape[1])]


def take_pieces(whole, pieces):
    me = lax.axis_index("ctx")
    for r, ref in enumerate(pieces):
        ref[...] = whole[at_block(me ^ r, ref.shape[0]), :]


def fetch(pairs, sems):
    copies = [pltpu.make_async_copy(source, target, sems.at[n]) for n, (source, target) in enumerate(pairs)]
    for copy in copies:
        copy.start()
    return copies


def prepare_kernel(*refs):
    *pieces, key_ref, value_ref, filter_ref, sems = refs[3:]
    for copy in fetch(list(zip(refs[:3], (key_ref, value_ref, filter_ref))), sems):
        copy.wait()
    me = lax.axis_index("ctx")
    for r, out_ref in enumerate(pieces):
        cols = at_block(me ^ r)
        mixed = key_ref[:, cols].astype(F32) * value_ref[:, cols].astype(F32)
        out_ref[:, pl.ds(0, LANES)] = mixed.astype(BF16)
        out_ref[:, pl.ds(LANES, LANES)] = filter_ref[cols, :].T.astype(BF16)


def forward_kernel(seqs, *refs):
    held, (matrix, turn), refs = refs[:seqs], refs[seqs : seqs + 2], refs[seqs + 3 :]
    sent, (spec_ref, whole, zh, zl, turned, conv) = refs[:seqs], refs[seqs:]
    blocks = spec_ref.shape[0] - 1
    place_pieces(held, whole)
    over_blocks(reader(whole), blocks, 2 * LANES, turn, zh, zl)
    for i in range(blocks + 1):
        spec = product3(matrix, zh[i], zl[i])
        spec_ref[i] = spec
        mixed_real, mixed_imag = spec[:LANES, :LANES], spec[LANES:, :LANES]
        filter_real, filter_imag = spec[:LANES, LANES:], spec[LANES:, LANES:]
        real = filter_real * mixed_real - filter_imag * mixed_imag
        imag = filter_real * mixed_imag + filter_imag * mixed_real
        turned[i] = product3(matrix, *split_bf16(jnp.concatenate([real, -imag], axis=0)))
    back_to_blocks(turned, blocks, LANES, turn, writer(conv))
    take_pieces(conv, sent)


def backward_kernel(seqs, *refs):
    held, (spec_ref, matrix, turn), refs = refs[:seqs], refs[seqs : seqs + 3], refs[seqs + 5 :]
    sent, (whole, zh, zl, turned, back) = refs[:seqs], refs[seqs:]
    blocks = spec_ref.shape[0] - 1
    place_pieces(held, whole)
    over_blocks(reader(whole), blocks, LANES, turn, zh, zl)
    for i in range(blocks + 1):
        grad = product3(matrix, zh[i], zl[i])
        grad_real, grad_imag = grad[:LANES], grad[LANES:]
        mixed_real, mixed_imag = spec_ref[i, :LANES, :LANES], spec_ref[i, LANES:, :LANES]
        filter_real, filter_imag = spec_ref[i, :LANES, LANES:], spec_ref[i, LANES:, LANES:]
        back_real = filter_real * grad_real + filter_imag * grad_imag
        back_imag = filter_imag * grad_real - filter_real * grad_imag
        taps_real = grad_real * mixed_real + grad_imag * mixed_imag
        taps_imag = grad_real * mixed_imag - grad_imag * mixed_real
        real = jnp.concatenate([back_real, taps_real], axis=1)
        imag = jnp.concatenate([back_imag, taps_imag], axis=1)
        turned[i] = product3(matrix, *split_bf16(jnp.concatenate([real, imag], axis=0)))
    back_to_blocks(turned, blocks, 2 * LANES, turn, writer(back))
    take_pieces(back, sent)


def gradient_kernel(parts, *refs):
    cots, (w_ref, query_ref), refs = refs[:parts], refs[parts : parts + 2], refs[parts + 3 :]
    gated_grad_ref, *pieces, cot = refs
    me, part = lax.axis_index("ctx"), lax.axis_index("tp")
    positions, width = cots[0].shape
    quarter = positions // parts
    total = None
    for r, ref in enumerate(cots):
        cot[part ^ r] = ref[...]
        term = lax.dot_general(
            ref[...], w_ref[:, at_block(part ^ r, width)], (((1,), (1,)), ((), ())), preferred_element_type=F32
        )
        total = term if total is None else total + term
    gated_grad_ref[...] = total
    for r, out_ref in enumerate(pieces):
        cols = at_block(me ^ r)
        out_ref[:, pl.ds(0, LANES)] = (gated_grad_ref[:, cols] * query_ref[:, cols].astype(F32)).astype(BF16)
        for k in range(width // LANES):
            out_ref[pl.ds(k * quarter, quarter), pl.ds(LANES, LANES)] = cot[
                me ^ r, at_block(part, quarter), pl.ds(k * LANES, LANES)
            ]


def quarter_kernel(seqs, *refs):
    held, out_ref = refs[:seqs], refs[-1]
    me = lax.axis_index("ctx")
    quarter = out_ref.shape[0] // seqs
    for r, ref in enumerate(held):
        for k in range(out_ref.shape[1] // LANES):
            out_ref[at_block(me ^ r, quarter), pl.ds(k * LANES, LANES)] = ref[
                pl.ds(k * quarter, quarter), pl.ds(LANES, LANES)
            ]


def output_kernel(seqs, *refs):
    held, (query_ref, gated_grad_ref, w_ref), refs = refs[:seqs], refs[seqs : seqs + 3], refs[seqs + 4 :]
    turned_ref, grad_query_ref, keep_ref, send_ref, whole = refs
    me, part = lax.axis_index("ctx"), lax.axis_index("tp")
    width = keep_ref.shape[2]
    for r, ref in enumerate(held):
        whole[:, at_block(me ^ r)] = ref[...]
    conv = whole[...].astype(F32)
    gated = query_ref[...].astype(F32) * conv
    turned_ref[...] = gated.T.astype(BF16)
    gated = gated.astype(BF16)
    grad_query_ref[...] = (gated_grad_ref[...] * conv).astype(BF16)
    for y in range(keep_ref.shape[0]):
        for ref, core in ((keep_ref, part & 1), (send_ref, (part & 1) ^ 1)):
            ref[y] = jnp.dot(gated, w_ref[:, at_block(2 * y + core, width)], preferred_element_type=F32)


def pair_kernel(keep_ref, other_ref, mine_ref, far_ref):
    y = lax.axis_index("tp") >> 1
    mine_ref[...] = keep_ref[y] + other_ref[y]
    far_ref[...] = (keep_ref[y ^ 1] + other_ref[y ^ 1]).astype(BF16)


def pass_kernel(one_ref, _, out_ref):
    out_ref[...] = one_ref[...]


def weight_kernel(seqs, *refs):
    pieces, cot_ref, (out_ref, cot) = refs[:seqs], refs[seqs], refs[-2:]
    me = lax.axis_index("ctx")
    parts = cot_ref.shape[0]
    quarter = cot_ref.shape[1] // parts
    total = None
    for r, ref in enumerate(pieces):
        for p in range(parts):
            cot[r, pl.ds(p * quarter, quarter), :] = cot_ref[p, at_block(me ^ r, quarter), :]
        term = jnp.dot(ref[...], cot[r], preferred_element_type=F32)
        total = term if total is None else total + term
    out_ref[...] = total.astype(BF16)


def mixed_kernel(seqs, *refs):
    held, (key_ref, value_ref, grad_key_ref, grad_value_ref, taps_ref) = refs[:seqs], refs[seqs:]
    me = lax.axis_index("ctx")
    for r, ref in enumerate(held):
        cols = at_block(me ^ r)
        mixed_grad = ref[:, pl.ds(0, LANES)].astype(F32)
        grad_key_ref[:, cols] = (mixed_grad * value_ref[:, cols].astype(F32)).astype(BF16)
        grad_value_ref[:, cols] = (mixed_grad * key_ref[:, cols].astype(F32)).astype(BF16)
        taps_ref[:, cols] = ref[:, pl.ds(LANES, LANES)]


def closing_kernel(factor, mine_ref, far_ref, weight_ref, weight_other, taps_ref, taps_other, *outs):
    output_ref, grad_wout_ref, grad_filter_ref = outs
    output_ref[...] = (mine_ref[...] + far_ref[...].astype(F32)).astype(BF16)
    grad_wout_ref[...] = (weight_ref[...].astype(F32) + weight_other[...].astype(F32)) * factor
    grad_filter_ref[...] = (taps_ref[...].astype(F32) + taps_other[...].astype(F32)).T * factor


def shape_of(shape, dtype):
    return jax.ShapeDtypeStruct(shape, dtype)


def call(kernel, outs, flops, moved, *args, scratch=(), left=(), room=20):
    vmem, anywhere = pl.BlockSpec(memory_space=pltpu.VMEM), pl.BlockSpec(memory_space=pl.ANY)
    return pl.pallas_call(
        kernel,
        out_shape=outs,
        in_specs=[anywhere if n in left else vmem for n in range(len(args))],
        out_specs=jax.tree.map(lambda _: vmem, outs),
        scratch_shapes=scratch,
        cost_estimate=pl.CostEstimate(flops=flops, bytes_accessed=moved, transcendentals=0),
        compiler_params=pltpu.CompilerParams(vmem_limit_bytes=room * 2**20),
    )(*args)


def exchange(pieces, axis):
    size = lax.axis_size(axis)
    return [pieces[0]] + [lax.ppermute(pieces[r], axis, [(d, d ^ r) for d in range(size)]) for r in range(1, size)]


def local_short(query_proj, key_proj, value_proj, filters, w_out, cotangent):
    query, key, value, cot = query_proj[0], key_proj[0], value_proj[0], cotangent[0]
    positions, channels = query.shape
    seqs, parts, pairs = lax.axis_size("ctx"), lax.axis_size("tp"), lax.axis_size("dp")
    blocks = positions * seqs // LANES
    features = w_out.shape[1]
    width = features // parts
    factor = 1.0 / math.sqrt(pairs * positions * seqs)
    tables = [jnp.asarray(m) for m in transform_tables(blocks)]
    ring = [(d, (d + 1) % pairs) for d in range(pairs)]
    table = (blocks + 1, 2 * LANES)
    one = [shape_of((positions, LANES), BF16)] * seqs
    two = [shape_of((positions, 2 * LANES), BF16)] * seqs
    rows = (positions, channels)
    line = seqs * positions

    over_chip, over_y = [[(j, j ^ r) for j in range(parts)] for r in (1, 2)]
    cot_far = lax.ppermute(cot, "tp", over_y)
    cot_rows = [cot, lax.ppermute(cot, "tp", over_chip), cot_far, lax.ppermute(cot_far, "tp", over_chip)]

    sent = call(
        prepare_kernel,
        two,
        10**6,
        2 * 10**6,
        key,
        value,
        filters,
        scratch=[
            pltpu.VMEM(rows, BF16),
            pltpu.VMEM(rows, BF16),
            pltpu.VMEM((channels, positions), F32),
            pltpu.SemaphoreType.DMA((3,)),
        ],
        left=(0, 1, 2),
        room=60,
    )
    held = exchange(sent, "ctx")

    gated_grad, *conv_grad = call(
        functools.partial(gradient_kernel, parts),
        [shape_of(rows, F32)] + two,
        2 * positions * channels * features,
        5 * 10**6,
        *cot_rows,
        w_out,
        query,
        sent[1],
        scratch=[pltpu.VMEM((parts, positions, width), BF16)],
        left=(parts + 2,),
    )
    grad_held = exchange(conv_grad, "ctx")

    *conv_sent, spec = call(
        functools.partial(forward_kernel, seqs),
        one + [shape_of(table + (2 * LANES,), F32)],
        10**9,
        9 * 10**6,
        *held,
        *tables,
        conv_grad[1],
        scratch=[
            pltpu.VMEM((line, 2 * LANES), BF16),
            pltpu.VMEM(table + (2 * LANES,), BF16),
            pltpu.VMEM(table + (2 * LANES,), BF16),
            pltpu.VMEM(table + (LANES,), F32),
            pltpu.VMEM((line, LANES), BF16),
        ],
        left=(seqs + 2,),
    )
    conv = exchange(conv_sent, "ctx")


    cot_quarters = call(
        functools.partial(quarter_kernel, seqs),
        shape_of((positions, width), BF16),
        10**6,
        10**6,
        *grad_held,
        conv_sent[1],
        left=(seqs,),
    )
    cot_cols = lax.all_gather(cot_quarters, "tp")
    back_sent = call(
        functools.partial(backward_kernel, seqs),
        two,
        10**9,
        9 * 10**6,
        *grad_held,
        spec,
        *tables,
        conv_sent[1],
        cot_quarters,
        scratch=[
            pltpu.VMEM((line, LANES), BF16),
            pltpu.VMEM(table + (LANES,), BF16),
            pltpu.VMEM(table + (LANES,), BF16),
            pltpu.VMEM(table + (2 * LANES,), F32),
            pltpu.VMEM((line, 2 * LANES), BF16),
        ],
        left=(seqs + 3, seqs + 4),
    )
    back = exchange(back_sent, "ctx")

    turned, grad_query, share_kept, share_sent = call(
        functools.partial(output_kernel, seqs),
        [shape_of((channels, positions), BF16), shape_of(rows, BF16)] + [shape_of((parts // 2, positions, width), F32)] * 2,
        2 * positions * channels * features,
        5 * 10**6,
        *conv,
        query,
        gated_grad,
        w_out,
        back_sent[1],
        scratch=[pltpu.VMEM(rows, BF16)],
        left=(seqs + 3,),
    )
    first, third = [[(d, d ^ r) for d in range(seqs)] for r in (1, 3)]
    across = lax.ppermute(turned, "ctx", third)
    near = lax.ppermute(turned, "ctx", first)
    passed = call(pass_kernel, shape_of((channels, positions), BF16), 10**6, 10**6, across, back[1], left=(1,))
    gathered = [turned, near, lax.ppermute(passed, "ctx", first), across]
    mine, far = call(
        pair_kernel,
        [shape_of((positions, width), F32), shape_of((positions, width), BF16)],
        10**6,
        3 * 10**6,
        share_kept,
        lax.ppermute(share_sent, "tp", [(j, j ^ 1) for j in range(parts)]),
    )
    far = lax.ppermute(far, "tp", [(j, j ^ 2) for j in range(parts)])

    grad_key, grad_value, taps = call(
        functools.partial(mixed_kernel, seqs),
        [shape_of(rows, BF16)] * 3,
        10**6,
        2 * 10**6,
        *back,
        key,
        value,
    )
    taps_other = lax.ppermute(taps, "dp", ring)
    weight_grad = call(
        functools.partial(weight_kernel, seqs),
        shape_of((channels, width), BF16),
        2 * line * channels * width,
        3 * 10**6,
        *gathered,
        cot_cols,
        back[2],
        left=(seqs + 1,),
        room=60,
        scratch=[pltpu.VMEM((seqs, positions, width), BF16)],
    )
    output, grad_wout, grad_filter = call(
        functools.partial(closing_kernel, factor),
        (shape_of((positions, width), BF16), shape_of((channels, width), F32), shape_of((channels, positions), F32)),
        10**6,
        5 * 10**6,
        mine,
        far,
        weight_grad,
        lax.ppermute(weight_grad, "dp", ring),
        taps,
        taps_other,
    )
    return (output[None], grad_query[None], grad_key[None], grad_value[None], grad_filter, grad_wout)


def local(*args):
    positions, channels = args[0].shape[1:]
    seqs, parts, pairs = lax.axis_size("ctx"), lax.axis_size("tp"), lax.axis_size("dp")
    short = (
        channels == seqs * LANES
        and positions % LANES == 0
        and args[4].shape[1] == parts * parts * LANES
        and positions * seqs <= 8 * LANES
        and seqs == parts == 4
        and pairs == 2
    )
    return (local_short if short else local_any_length)(*args)


def solution(mesh):
    in_specs = (
        P("dp", "ctx", "tp"),
        P("dp", "ctx", "tp"),
        P("dp", "ctx", "tp"),
        P("tp", "ctx"),
        P("tp", None),
        P("dp", "ctx", "tp"),
    )
    out_specs = (
        P("dp", "ctx", "tp"),
        P("dp", "ctx", "tp"),
        P("dp", "ctx", "tp"),
        P("dp", "ctx", "tp"),
        P("tp", "ctx"),
        P("tp", "ctx"),
    )
    return jax.shard_map(local, mesh=mesh, in_specs=in_specs, out_specs=out_specs, check_vma=False)
```

```python
import functools
import math

import jax
import jax.numpy as jnp
import ml_dtypes
import numpy as np
from jax import lax
from jax.experimental import pallas as pl
from jax.experimental.pallas import tpu as pltpu
from jax.sharding import PartitionSpec as P

F32 = jnp.float32
BF16 = jnp.bfloat16
LANES = 128
ROWS = 16


def build_tables(length_fft):
    blocks = length_fft // 128
    outer = jnp.arange(blocks, dtype=jnp.int32)
    inner = jnp.arange(blocks // 2, dtype=jnp.int32)
    column = jnp.arange(128, dtype=jnp.int32)
    first = (outer[:, None] * inner[None, :] % blocks).astype(jnp.float32) * (
        -2.0 * math.pi / blocks
    )
    turned = (outer[:, None] * column[None, :] % length_fft).astype(jnp.float32) * (
        -2.0 * math.pi / length_fft
    )
    second = (column[:, None] * column[None, :] % 128).astype(jnp.float32) * (-2.0 * math.pi / 128)
    return (
        jnp.cos(first),
        jnp.sin(first),
        jnp.cos(turned),
        jnp.sin(turned),
        jnp.cos(second),
        jnp.sin(second),
    )


def product(form, left, right):
    return jnp.einsum(form, left, right, precision=lax.Precision.HIGHEST)


def forward_transform(signal, tables):
    cos_first, sin_first, cos_turn, sin_turn, cos_second, sin_second = tables
    real_one = product("ia,cab->cib", cos_first, signal)
    imag_one = product("ia,cab->cib", sin_first, signal)
    real_two = real_one * cos_turn - imag_one * sin_turn
    imag_two = real_one * sin_turn + imag_one * cos_turn
    real_out = product("cib,bj->cij", real_two, cos_second) - product(
        "cib,bj->cij", imag_two, sin_second
    )
    imag_out = product("cib,bj->cij", real_two, sin_second) + product(
        "cib,bj->cij", imag_two, cos_second
    )
    return (real_out, imag_out)


def inverse_transform(real_in, imag_in, tables, length_fft):
    cos_first, sin_first, cos_turn, sin_turn, cos_second, sin_second = tables
    real_one = product("cij,jb->cib", real_in, cos_second) + product(
        "cij,jb->cib", imag_in, sin_second
    )
    imag_one = product("cij,jb->cib", imag_in, cos_second) - product(
        "cij,jb->cib", real_in, sin_second
    )
    real_two = real_one * cos_turn + imag_one * sin_turn
    imag_two = imag_one * cos_turn - real_one * sin_turn
    result = product("ia,cib->cab", cos_first, real_two) + product(
        "ia,cib->cab", sin_first, imag_two
    )
    return result / length_fft


def local_any_length(query_proj, key_proj, value_proj, filters, w_out, cotangent):
    query_rows = query_proj[0].astype(jnp.float32)
    key_rows = key_proj[0].astype(jnp.float32)
    value_rows = value_proj[0].astype(jnp.float32)
    positions, channels = query_rows.shape
    seq_devices = lax.axis_size("ctx")
    length_fft = 2 * positions * seq_devices
    tables = build_tables(length_fft)
    mixed = (key_rows * value_rows).T
    mixed_chan, filter_chan = (
        lax.all_to_all(mixed, "ctx", split_axis=0, concat_axis=1, tiled=True),
        lax.all_to_all(filters, "ctx", split_axis=0, concat_axis=1, tiled=True),
    )
    local_channels = mixed_chan.shape[0]
    block_shape = (local_channels, length_fft // 256, 128)
    mixed_real, mixed_imag = forward_transform(mixed_chan.reshape(block_shape), tables)
    filter_real, filter_imag = forward_transform(filter_chan.reshape(block_shape), tables)
    conv_real = filter_real * mixed_real - filter_imag * mixed_imag
    conv_imag = filter_real * mixed_imag + filter_imag * mixed_real
    conv_chan = inverse_transform(conv_real, conv_imag, tables, length_fft).reshape(
        local_channels, -1
    )
    conv_back = lax.all_to_all(conv_chan, "ctx", split_axis=1, concat_axis=0, tiled=True)
    conv = conv_back.T
    gated = (query_rows * conv).astype(jnp.bfloat16)
    partial_terms = jnp.dot(gated, w_out, preferred_element_type=jnp.float32)
    output = lax.psum_scatter(partial_terms, "tp", scatter_dimension=1, tiled=True).astype(
        jnp.bfloat16
    )
    piece = lax.all_gather(cotangent[0], "tp", axis=1, tiled=True)
    grad_gated = lax.dot_general(
        piece, w_out, (((1,), (1,)), ((), ())), preferred_element_type=jnp.float32
    )
    weight_piece = lax.dot_general(
        gated, piece, (((0,), (0,)), ((), ())), preferred_element_type=jnp.float32
    )
    weight_grad = weight_piece
    grad_gated, weight_grad = (grad_gated, weight_grad)
    grad_query = (grad_gated * conv).astype(jnp.bfloat16)
    grad_conv = (grad_gated * query_rows).T
    grad_chan = lax.all_to_all(grad_conv, "ctx", split_axis=0, concat_axis=1, tiled=True)
    grad_real, grad_imag = forward_transform(grad_chan.reshape(block_shape), tables)
    back_real = filter_real * grad_real + filter_imag * grad_imag
    back_imag = filter_real * grad_imag - filter_imag * grad_real
    taps_real = grad_real * mixed_real + grad_imag * mixed_imag
    taps_imag = grad_imag * mixed_real - grad_real * mixed_imag
    mixed_grad_chan = inverse_transform(back_real, back_imag, tables, length_fft).reshape(
        local_channels, -1
    )
    filter_grad_chan = inverse_transform(taps_real, taps_imag, tables, length_fft).reshape(
        local_channels, -1
    )
    mixed_grad_back, filter_grad_back = (
        lax.all_to_all(mixed_grad_chan, "ctx", split_axis=1, concat_axis=0, tiled=True),
        lax.all_to_all(filter_grad_chan, "ctx", split_axis=1, concat_axis=0, tiled=True),
    )
    grad_mixed = mixed_grad_back.T
    grad_key = (grad_mixed * value_rows).astype(jnp.bfloat16)
    grad_value = (grad_mixed * key_rows).astype(jnp.bfloat16)
    factor = 1.0 / math.sqrt(lax.axis_size("dp") * positions * seq_devices)
    grad_filter = lax.psum(filter_grad_back, "dp") * factor
    summed_seq = lax.psum_scatter(weight_grad, "ctx", scatter_dimension=1, tiled=True)
    summed_weight = lax.psum(summed_seq, "dp")
    grad_wout = summed_weight * factor
    return (
        output[None],
        grad_query[None],
        grad_key[None],
        grad_value[None],
        grad_filter,
        grad_wout,
    )


@functools.lru_cache
def transform_tables(blocks):
    length_fft = 2 * blocks * LANES
    b = np.arange(LANES, dtype=np.int64)
    angle = (2.0 * math.pi / LANES) * (b[:, None] * b[None, :] % LANES)
    cos, sin = np.cos(angle), np.sin(angle)
    whole = np.block([[cos, sin], [-sin, cos]])
    high = whole.astype(ml_dtypes.bfloat16)
    low = (whole - high.astype(np.float64)).astype(ml_dtypes.bfloat16)
    turn = np.zeros((LANES, LANES))
    i = np.arange(blocks + 1)
    angle = (2.0 * math.pi / length_fft) * (b[:, None] * i[None, :] % length_fft)
    turn[:, : blocks + 1] = np.cos(angle)
    turn[:, LANES // 2 : LANES // 2 + blocks + 1] = np.sin(angle)
    return np.stack([high, low]), turn.astype(np.float32)


def scaled_sum(terms):
    total = None
    for factor, term in terms:
        if abs(factor) < 1e-9:
            continue
        if abs(factor - 1.0) < 1e-9:
            total = term if total is None else total + term
        elif abs(factor + 1.0) < 1e-9:
            total = -term if total is None else total - term
        else:
            total = factor * term if total is None else total + factor * term
    return total


def split_bf16(value):
    high = value.astype(BF16)
    return high, (value - high.astype(F32)).astype(BF16)


def product3(matrix_ref, high, low):
    dot = functools.partial(jnp.dot, preferred_element_type=F32)
    return dot(matrix_ref[0], high) + (dot(matrix_ref[0], low) + dot(matrix_ref[1], high))


def turn_of(turn_ref, i, row):
    rows = pl.ds(row, ROWS)
    cos = turn_ref[rows, i : i + 1]
    sin = turn_ref[rows, LANES // 2 + i : LANES // 2 + i + 1]
    return jnp.broadcast_to(cos, (ROWS, LANES)), jnp.broadcast_to(sin, (ROWS, LANES))


def each_chunk(lanes, body):
    @pl.loop(0, LANES // ROWS, unroll=4)
    def _(step):
        for lane in range(0, lanes, LANES):
            body(pl.multiple_of(step * ROWS, ROWS), lane)


def over_blocks(read, blocks, lanes, turn_ref, high, low):
    def chunk(row, lane):
        def put(i, real, imag):
            if i > 0:
                cos, sin = turn_of(turn_ref, i, row)
                if imag is None:
                    real, imag = real * cos, -(real * sin)
                else:
                    real, imag = real * cos + imag * sin, imag * cos - real * sin
            for part, value in ((0, real), (1, jnp.zeros_like(real) if imag is None else imag)):
                top, rest = split_bf16(value)
                rows = pl.ds(pl.multiple_of(part * LANES + row, ROWS), ROWS)
                high[i, rows, pl.ds(lane, LANES)] = top
                low[i, rows, pl.ds(lane, LANES)] = rest

        slabs = [read(a, row, lane) for a in range(blocks)]
        for i in range(blocks // 2 + 1):
            sums = []
            for first in (0, 1):
                picked = range(first, blocks, 2)
                angle = [math.pi * ((i * a) % (2 * blocks)) / blocks for a in picked]
                sums.append(scaled_sum([(math.cos(g), slabs[a]) for g, a in zip(angle, picked)]))
                sums.append(scaled_sum([(-math.sin(g), slabs[a]) for g, a in zip(angle, picked)]))
            even_real, even_imag, odd_real, odd_imag = sums

            def joined(one, other, sign):
                if one is None or other is None:
                    return one if other is None else (other if sign > 0 else -other)
                return one + other if sign > 0 else one - other

            put(i, joined(even_real, odd_real, 1), joined(even_imag, odd_imag, 1))
            if blocks - i != i:
                put(blocks - i, joined(even_real, odd_real, -1), joined(odd_imag, even_imag, -1))

    each_chunk(lanes, chunk)


def back_to_blocks(turned, blocks, lanes, turn_ref, write):
    scale = 1.0 / (blocks * LANES)

    def chunk(row, lane):
        def get(i):
            real = turned[i, pl.ds(row, ROWS), pl.ds(lane, LANES)]
            imag = -turned[i, pl.ds(pl.multiple_of(LANES + row, ROWS), ROWS), pl.ds(lane, LANES)]
            if i > 0:
                cos, sin = turn_of(turn_ref, i, row)
                real, imag = real * cos - imag * sin, imag * cos + real * sin
            return real, imag

        terms = [[] for _ in range(blocks)]
        for i in range(blocks // 2 + 1):
            real, imag = get(i)
            if blocks - i != i:
                other_real, other_imag = get(blocks - i)
                pairs = ((real + other_real, imag - other_imag), (real - other_real, imag + other_imag))
            else:
                pairs = ((real, imag), (real, imag))
            if i == 0:
                pairs = tuple((0.5 * one, 0.5 * two) for one, two in pairs)
            for a in range(blocks):
                angle = math.pi * ((i * a) % (2 * blocks)) / blocks
                terms[a].append((math.cos(angle), pairs[a % 2][0]))
                terms[a].append((-math.sin(angle), pairs[a % 2][1]))
        for a in range(blocks):
            write(a, row, lane, scaled_sum(terms[a]) * scale)

    each_chunk(lanes, chunk)


def at_block(index, size=LANES):
    return pl.ds(pl.multiple_of(index * size, size), size)


def reader(ref):
    def read(a, row, lane):
        rows = pl.ds(pl.multiple_of(a * LANES + row, ROWS), ROWS)
        return ref[rows, pl.ds(lane, LANES)].astype(F32)

    return read


def writer(ref):
    def write(a, row, lane, value):
        rows = pl.ds(pl.multiple_of(a * LANES + row, ROWS), ROWS)
        ref[rows, pl.ds(lane, LANES)] = value.astype(ref.dtype)

    return write


def place_pieces(pieces, whole):
    me = lax.axis_index("ctx")
    for r, ref in enumerate(pieces):
        whole[at_block(me ^ r, ref.shape[0]), :] = ref[:, pl.ds(0, whole.shape[1])]


def take_pieces(whole, pieces):
    me = lax.axis_index("ctx")
    for r, ref in enumerate(pieces):
        ref[...] = whole[at_block(me ^ r, ref.shape[0]), :]


def fetch(pairs, sems):
    copies = [pltpu.make_async_copy(source, target, sems.at[n]) for n, (source, target) in enumerate(pairs)]
    for copy in copies:
        copy.start()
    return copies


def prepare_kernel(*refs):
    *pieces, key_ref, value_ref, filter_ref, sems = refs[3:]
    for copy in fetch(list(zip(refs[:3], (key_ref, value_ref, filter_ref))), sems):
        copy.wait()
    me = lax.axis_index("ctx")
    for r, out_ref in enumerate(pieces):
        cols = at_block(me ^ r)
        mixed = key_ref[:, cols].astype(F32) * value_ref[:, cols].astype(F32)
        out_ref[:, pl.ds(0, LANES)] = mixed.astype(BF16)
        out_ref[:, pl.ds(LANES, LANES)] = filter_ref[cols, :].T.astype(BF16)


def forward_kernel(seqs, *refs):
    held, (matrix, turn), refs = refs[:seqs], refs[seqs : seqs + 2], refs[seqs + 3 :]
    sent, (spec_ref, whole, zh, zl, turned, conv) = refs[:seqs], refs[seqs:]
    blocks = spec_ref.shape[0] - 1
    place_pieces(held, whole)
    over_blocks(reader(whole), blocks, 2 * LANES, turn, zh, zl)
    for i in range(blocks + 1):
        spec = product3(matrix, zh[i], zl[i])
        spec_ref[i] = spec
        mixed_real, mixed_imag = spec[:LANES, :LANES], spec[LANES:, :LANES]
        filter_real, filter_imag = spec[:LANES, LANES:], spec[LANES:, LANES:]
        real = filter_real * mixed_real - filter_imag * mixed_imag
        imag = filter_real * mixed_imag + filter_imag * mixed_real
        turned[i] = product3(matrix, *split_bf16(jnp.concatenate([real, -imag], axis=0)))
    back_to_blocks(turned, blocks, LANES, turn, writer(conv))
    take_pieces(conv, sent)


def backward_kernel(seqs, *refs):
    held, (spec_ref, matrix, turn), refs = refs[:seqs], refs[seqs : seqs + 3], refs[seqs + 5 :]
    sent, (whole, zh, zl, turned, back) = refs[:seqs], refs[seqs:]
    blocks = spec_ref.shape[0] - 1
    place_pieces(held, whole)
    over_blocks(reader(whole), blocks, LANES, turn, zh, zl)
    for i in range(blocks + 1):
        grad = product3(matrix, zh[i], zl[i])
        grad_real, grad_imag = grad[:LANES], grad[LANES:]
        mixed_real, mixed_imag = spec_ref[i, :LANES, :LANES], spec_ref[i, LANES:, :LANES]
        filter_real, filter_imag = spec_ref[i, :LANES, LANES:], spec_ref[i, LANES:, LANES:]
        back_real = filter_real * grad_real + filter_imag * grad_imag
        back_imag = filter_imag * grad_real - filter_real * grad_imag
        taps_real = grad_real * mixed_real + grad_imag * mixed_imag
        taps_imag = grad_real * mixed_imag - grad_imag * mixed_real
        real = jnp.concatenate([back_real, taps_real], axis=1)
        imag = jnp.concatenate([back_imag, taps_imag], axis=1)
        turned[i] = product3(matrix, *split_bf16(jnp.concatenate([real, imag], axis=0)))
    back_to_blocks(turned, blocks, 2 * LANES, turn, writer(back))
    take_pieces(back, sent)


def gradient_kernel(parts, *refs):
    cots, (w_ref, query_ref), refs = refs[:parts], refs[parts : parts + 2], refs[parts + 3 :]
    gated_grad_ref, *pieces, cot = refs
    me, part = lax.axis_index("ctx"), lax.axis_index("tp")
    positions, width = cots[0].shape
    quarter = positions // parts
    total = None
    for r, ref in enumerate(cots):
        cot[part ^ r] = ref[...]
        term = lax.dot_general(
            ref[...], w_ref[:, at_block(part ^ r, width)], (((1,), (1,)), ((), ())), preferred_element_type=F32
        )
        total = term if total is None else total + term
    gated_grad_ref[...] = total
    for r, out_ref in enumerate(pieces):
        cols = at_block(me ^ r)
        out_ref[:, pl.ds(0, LANES)] = (gated_grad_ref[:, cols] * query_ref[:, cols].astype(F32)).astype(BF16)
        for k in range(width // LANES):
            out_ref[pl.ds(k * quarter, quarter), pl.ds(LANES, LANES)] = cot[
                me ^ r, at_block(part, quarter), pl.ds(k * LANES, LANES)
            ]


def quarter_kernel(seqs, *refs):
    held, out_ref = refs[:seqs], refs[-1]
    me = lax.axis_index("ctx")
    quarter = out_ref.shape[0] // seqs
    for r, ref in enumerate(held):
        for k in range(out_ref.shape[1] // LANES):
            out_ref[at_block(me ^ r, quarter), pl.ds(k * LANES, LANES)] = ref[
                pl.ds(k * quarter, quarter), pl.ds(LANES, LANES)
            ]


def output_kernel(seqs, *refs):
    held, (query_ref, gated_grad_ref, w_ref), refs = refs[:seqs], refs[seqs : seqs + 3], refs[seqs + 4 :]
    turned_ref, grad_query_ref, keep_ref, send_ref, whole = refs
    me, part = lax.axis_index("ctx"), lax.axis_index("tp")
    width = keep_ref.shape[2]
    for r, ref in enumerate(held):
        whole[:, at_block(me ^ r)] = ref[...]
    conv = whole[...].astype(F32)
    gated = query_ref[...].astype(F32) * conv
    turned_ref[...] = gated.T.astype(BF16)
    gated = gated.astype(BF16)
    grad_query_ref[...] = (gated_grad_ref[...] * conv).astype(BF16)
    for y in range(keep_ref.shape[0]):
        for ref, core in ((keep_ref, part & 1), (send_ref, (part & 1) ^ 1)):
            ref[y] = jnp.dot(gated, w_ref[:, at_block(2 * y + core, width)], preferred_element_type=F32)


def pair_kernel(keep_ref, other_ref, mine_ref, far_ref):
    y = lax.axis_index("tp") >> 1
    mine_ref[...] = keep_ref[y] + other_ref[y]
    far_ref[...] = (keep_ref[y ^ 1] + other_ref[y ^ 1]).astype(BF16)


def pass_kernel(one_ref, _, out_ref):
    out_ref[...] = one_ref[...]


def weight_kernel(seqs, *refs):
    pieces, cot_ref, (out_ref, cot) = refs[:seqs], refs[seqs], refs[-2:]
    me = lax.axis_index("ctx")
    parts = cot_ref.shape[0]
    quarter = cot_ref.shape[1] // parts
    total = None
    for r, ref in enumerate(pieces):
        for p in range(parts):
            cot[r, pl.ds(p * quarter, quarter), :] = cot_ref[p, at_block(me ^ r, quarter), :]
        term = jnp.dot(ref[...], cot[r], preferred_element_type=F32)
        total = term if total is None else total + term
    out_ref[...] = total.astype(BF16)


def mixed_kernel(seqs, *refs):
    held, (key_ref, value_ref, grad_key_ref, grad_value_ref, taps_ref) = refs[:seqs], refs[seqs:]
    me = lax.axis_index("ctx")
    for r, ref in enumerate(held):
        cols = at_block(me ^ r)
        mixed_grad = ref[:, pl.ds(0, LANES)].astype(F32)
        grad_key_ref[:, cols] = (mixed_grad * value_ref[:, cols].astype(F32)).astype(BF16)
        grad_value_ref[:, cols] = (mixed_grad * key_ref[:, cols].astype(F32)).astype(BF16)
        taps_ref[:, cols] = ref[:, pl.ds(LANES, LANES)]


def closing_kernel(factor, mine_ref, far_ref, weight_ref, weight_other, taps_ref, taps_other, *outs):
    output_ref, grad_wout_ref, grad_filter_ref = outs
    output_ref[...] = (mine_ref[...] + far_ref[...].astype(F32)).astype(BF16)
    grad_wout_ref[...] = (weight_ref[...].astype(F32) + weight_other[...].astype(F32)) * factor
    grad_filter_ref[...] = (taps_ref[...].astype(F32) + taps_other[...].astype(F32)).T * factor


def shape_of(shape, dtype):
    return jax.ShapeDtypeStruct(shape, dtype)


def call(kernel, outs, flops, moved, *args, scratch=(), left=(), room=20):
    vmem, anywhere = pl.BlockSpec(memory_space=pltpu.VMEM), pl.BlockSpec(memory_space=pl.ANY)
    return pl.pallas_call(
        kernel,
        out_shape=outs,
        in_specs=[anywhere if n in left else vmem for n in range(len(args))],
        out_specs=jax.tree.map(lambda _: vmem, outs),
        scratch_shapes=scratch,
        cost_estimate=pl.CostEstimate(flops=flops, bytes_accessed=moved, transcendentals=0),
        compiler_params=pltpu.CompilerParams(vmem_limit_bytes=room * 2**20),
    )(*args)


def exchange(pieces, axis):
    size = lax.axis_size(axis)
    return [pieces[0]] + [lax.ppermute(pieces[r], axis, [(d, d ^ r) for d in range(size)]) for r in range(1, size)]


def local_short(query_proj, key_proj, value_proj, filters, w_out, cotangent):
    query, key, value, cot = query_proj[0], key_proj[0], value_proj[0], cotangent[0]
    positions, channels = query.shape
    seqs, parts, pairs = lax.axis_size("ctx"), lax.axis_size("tp"), lax.axis_size("dp")
    blocks = positions * seqs // LANES
    features = w_out.shape[1]
    width = features // parts
    factor = 1.0 / math.sqrt(pairs * positions * seqs)
    tables = [jnp.asarray(m) for m in transform_tables(blocks)]
    ring = [(d, (d + 1) % pairs) for d in range(pairs)]
    table = (blocks + 1, 2 * LANES)
    one = [shape_of((positions, LANES), BF16)] * seqs
    two = [shape_of((positions, 2 * LANES), BF16)] * seqs
    rows = (positions, channels)
    line = seqs * positions

    over_chip, over_y = [[(j, j ^ r) for j in range(parts)] for r in (1, 2)]
    cot_core, cot_far = lax.ppermute(cot, "tp", over_chip), lax.ppermute(cot, "tp", over_y)

    sent = call(
        prepare_kernel,
        two,
        10**6,
        2 * 10**6,
        key,
        value,
        filters,
        scratch=[
            pltpu.VMEM(rows, BF16),
            pltpu.VMEM(rows, BF16),
            pltpu.VMEM((channels, positions), F32),
            pltpu.SemaphoreType.DMA((3,)),
        ],
        left=(0, 1, 2),
        room=60,
    )
    held = exchange(sent, "ctx")
    far_passed = call(pass_kernel, shape_of(rows, BF16), 10**6, 10**6, cot_far, sent[1], left=(1,))
    cot_rows = [cot, cot_core, cot_far, lax.ppermute(far_passed, "tp", over_chip)]

    gated_grad, *conv_grad = call(
        functools.partial(gradient_kernel, parts),
        [shape_of(rows, F32)] + two,
        2 * positions * channels * features,
        5 * 10**6,
        *cot_rows,
        w_out,
        query,
        sent[1],
        scratch=[pltpu.VMEM((parts, positions, width), BF16)],
        left=(parts + 2,),
    )
    grad_held = exchange(conv_grad, "ctx")

    *conv_sent, spec = call(
        functools.partial(forward_kernel, seqs),
        one + [shape_of(table + (2 * LANES,), F32)],
        10**9,
        9 * 10**6,
        *held,
        *tables,
        conv_grad[1],
        scratch=[
            pltpu.VMEM((line, 2 * LANES), BF16),
            pltpu.VMEM(table + (2 * LANES,), BF16),
            pltpu.VMEM(table + (2 * LANES,), BF16),
            pltpu.VMEM(table + (LANES,), F32),
            pltpu.VMEM((line, LANES), BF16),
        ],
        left=(seqs + 2,),
    )
    conv = exchange(conv_sent, "ctx")


    cot_quarters = call(
        functools.partial(quarter_kernel, seqs),
        shape_of((positions, width), BF16),
        10**6,
        10**6,
        *grad_held,
        conv_sent[1],
        left=(seqs,),
    )
    cot_cols = lax.all_gather(cot_quarters, "tp")
    back_sent = call(
        functools.partial(backward_kernel, seqs),
        two,
        10**9,
        9 * 10**6,
        *grad_held,
        spec,
        *tables,
        conv_sent[1],
        cot_quarters,
        scratch=[
            pltpu.VMEM((line, LANES), BF16),
            pltpu.VMEM(table + (LANES,), BF16),
            pltpu.VMEM(table + (LANES,), BF16),
            pltpu.VMEM(table + (2 * LANES,), F32),
            pltpu.VMEM((line, 2 * LANES), BF16),
        ],
        left=(seqs + 3, seqs + 4),
    )
    back = exchange(back_sent, "ctx")

    turned, grad_query, share_kept, share_sent = call(
        functools.partial(output_kernel, seqs),
        [shape_of((channels, positions), BF16), shape_of(rows, BF16)] + [shape_of((parts // 2, positions, width), F32)] * 2,
        2 * positions * channels * features,
        5 * 10**6,
        *conv,
        query,
        gated_grad,
        w_out,
        back_sent[1],
        scratch=[pltpu.VMEM(rows, BF16)],
        left=(seqs + 3,),
    )
    first, third = [[(d, d ^ r) for d in range(seqs)] for r in (1, 3)]
    across = lax.ppermute(turned, "ctx", third)
    near = lax.ppermute(turned, "ctx", first)
    passed = call(pass_kernel, shape_of((channels, positions), BF16), 10**6, 10**6, across, back[1], left=(1,))
    gathered = [turned, near, lax.ppermute(passed, "ctx", first), across]
    mine, far = call(
        pair_kernel,
        [shape_of((positions, width), F32), shape_of((positions, width), BF16)],
        10**6,
        3 * 10**6,
        share_kept,
        lax.ppermute(share_sent, "tp", [(j, j ^ 1) for j in range(parts)]),
    )
    far = lax.ppermute(far, "tp", [(j, j ^ 2) for j in range(parts)])

    grad_key, grad_value, taps = call(
        functools.partial(mixed_kernel, seqs),
        [shape_of(rows, BF16)] * 3,
        10**6,
        2 * 10**6,
        *back,
        key,
        value,
    )
    taps_other = lax.ppermute(taps, "dp", ring)
    weight_grad = call(
        functools.partial(weight_kernel, seqs),
        shape_of((channels, width), BF16),
        2 * line * channels * width,
        3 * 10**6,
        *gathered,
        cot_cols,
        back[2],
        left=(seqs + 1,),
        room=60,
        scratch=[pltpu.VMEM((seqs, positions, width), BF16)],
    )
    output, grad_wout, grad_filter = call(
        functools.partial(closing_kernel, factor),
        (shape_of((positions, width), BF16), shape_of((channels, width), F32), shape_of((channels, positions), F32)),
        10**6,
        5 * 10**6,
        mine,
        far,
        weight_grad,
        lax.ppermute(weight_grad, "dp", ring),
        taps,
        taps_other,
    )
    return (output[None], grad_query[None], grad_key[None], grad_value[None], grad_filter, grad_wout)


def local(*args):
    positions, channels = args[0].shape[1:]
    seqs, parts, pairs = lax.axis_size("ctx"), lax.axis_size("tp"), lax.axis_size("dp")
    short = (
        channels == seqs * LANES
        and positions % LANES == 0
        and args[4].shape[1] == parts * parts * LANES
        and positions * seqs <= 8 * LANES
        and seqs == parts == 4
        and pairs == 2
    )
    return (local_short if short else local_any_length)(*args)


def solution(mesh):
    in_specs = (
        P("dp", "ctx", "tp"),
        P("dp", "ctx", "tp"),
        P("dp", "ctx", "tp"),
        P("tp", "ctx"),
        P("tp", None),
        P("dp", "ctx", "tp"),
    )
    out_specs = (
        P("dp", "ctx", "tp"),
        P("dp", "ctx", "tp"),
        P("dp", "ctx", "tp"),
        P("dp", "ctx", "tp"),
        P("tp", "ctx"),
        P("tp", "ctx"),
    )
    return jax.shard_map(local, mesh=mesh, in_specs=in_specs, out_specs=out_specs, check_vma=False)
```
